32 devices in a mesh: groups: 2 (over y), slab: 4 (over z), orb: 4 (over x, core).
Axes of the slice: x: 2, y: 2, z: 4, core: 2. Of those that a mesh axis runs over, the one named last changes fastest.
Arguments:
- fractions: float32 [3, 3072], P(None, ('groups', 'slab', 'orb')), parts along dimension 1, may hold values from 0 to 1
- cell_index: int32 [2, 3072], P(None, ('groups', 'slab', 'orb')), parts along dimension 1, may hold values from 0 to 15
- slab_owner: int32 [3072, 1], P(('groups', 'slab', 'orb')), parts along dimension 0, may hold values from 0 to 3; in each aligned block of 96 rows (0 to 95, 96 to 191, ...) at most 30 rows name the same one
- spline_table: float32 [4, 16, 16, 4, 2048], P('slab', None, None, None, 'orb'), may hold values from -6 to 6
Outputs:
- orbital_values: bfloat16 [5, 3072, 2048], P(None, ('groups', 'slab', 'orb')), parts along dimension 1
The draws below stay inside these ranges and needn't reach their ends.
There are 2 independent parts, one for each index of `groups`. The reference program is written for one: setup_inputs(seed, part) draws one part's arguments, and reference() takes and returns one part's arrays. A program takes and returns all parts, laid end to end along the dimension named above; an argument that names none is the same for every part. Nothing has to cross between parts.
Inputs may be any that keep to these rules, and one draw needn't show every extreme that they name: `slab_owner`: in each aligned block of 96 electrons (the electrons of one device) at most 30 name the same slab, a bound that some block reaches of them.
All inputs are finite; a program needn't handle non-finite values.
Results may differ from the reference program's by a relative error of at most 0.001.
Values may be sent and summed in bfloat16 or wider, within the bound.
No kernel may reach another device: no remote copies, remote signals or barrier semaphores. Data moves between devices by JAX's collectives and lax.ppermute only.
A program may use at most 64 MiB of HBM per device.

```python
import math
import jax
import jax.numpy as jnp
import numpy as np
from jax import lax

ORBS = 2048
GW = 16
E_DEV = 96
CAPO = 30
ELEC = 1536
N_SLAB = 4


def place_ends(array, key, smallest, high):
    index_at = [jax.random.randint(jax.random.fold_in(key, axis), (), 0, length) for axis, length in enumerate(array.shape)]
    main_axis = array.shape.index(max(array.shape))
    next_to = index_at[:main_axis] + [(index_at[main_axis] + 1) % array.shape[main_axis]] + index_at[main_axis + 1:]
    return array.at[tuple(index_at)].set(smallest).at[tuple(next_to)].set(high)


def levels(rng, dims, shards, smallest, high):
    loudness, own = 1.0, jax.random.fold_in(rng, 6)
    for axis_at, blocks in shards:
        steps = jnp.exp(jax.random.uniform(jax.random.fold_in(own, axis_at), (blocks,), jnp.float32, smallest / len(shards), high / len(shards)))
        loudness = loudness * jnp.repeat(steps, dims[axis_at] // blocks).reshape([-1 if axis == axis_at else 1 for axis in range(len(dims))])
    return loudness


def shared_out(own_key, own, number, rows, amount, top, limit, slope):
    ranking = jax.random.permutation(own_key, amount)
    heavy_load, usual = shares(amount, rows * top, limit, slope, True), shares(amount, rows * top, limit, slope, False)
    places = jnp.arange(amount)

    def named(tallies, rotation):
        used = int((tallies > 0).sum())
        fixed = max(1, used // 4)
        shifted = fixed + (places - fixed + rotation * (used - fixed)) % max(1, amount - fixed)
        return jnp.zeros((amount,), jnp.int32).at[ranking[jnp.where(places < fixed, places, shifted)]].set(jnp.asarray(tallies, jnp.int32))

    tallies = jnp.where(number % 4 == 0, named(heavy_load, number // 4), named(usual, number - number // 4 - 1))
    mixed = jax.random.permutation(jax.random.fold_in(own, 3), amount)
    source_of, taker = mixed[0:amount // 2 * 2:2], mixed[1:amount // 2 * 2:2]
    slack = jnp.minimum(tallies[source_of] - 1, limit - tallies[taker]) // 2
    slack = jnp.where((source_of == ranking[0]) | (taker == ranking[0]) | (tallies[taker] == 0), 0, jnp.maximum(slack, 0))
    shifted = jax.random.randint(jax.random.fold_in(own, 4), (amount // 2,), 0, 1 << 20) % (slack + 1)
    tallies = tallies.at[source_of].add(-shifted).at[taker].add(shifted)
    members = jnp.searchsorted(jnp.cumsum(tallies), jnp.arange(rows * top), side="right").astype(jnp.int32)
    listing = members.reshape(top, rows).T
    listing = listing[jax.random.permutation(jax.random.fold_in(own, 1), rows)]
    rotation = jax.random.randint(jax.random.fold_in(own, 2), (rows, 1), 0, top)
    return jnp.take_along_axis(listing, (jnp.arange(top)[None, :] + rotation) % top, axis=1)


def shares(amount, total, most, slope, full):
    loads = [(1 << 20) // math.isqrt(rank ** slope) + 1 for rank in range(1, amount + 1)]
    largest = most if full else min(most, max(-(-total // amount), total * loads[0] // sum(loads)))
    least = 1 if total - largest >= amount - 1 else 0
    counts, surplus = [largest] + [least] * (amount - 1), total - largest - least * (amount - 1)
    while surplus > 0:
        candidates = [i for i in range(1, amount) if counts[i] < largest] or [i for i in range(1, amount) if counts[i] < most]
        pool, budget = sum([loads[i] for i in candidates]), surplus
        for i in candidates:
            more = min(most - counts[i], max(1, budget * loads[i] // pool), surplus)
            counts[i] = counts[i] + more
            surplus = surplus - more
    return np.array(counts)


def normal_values(rng, extent, spread, reach, shards=(), kind=jnp.bfloat16):
    values = jax.random.normal(rng, extent, jnp.float32) * spread
    if len(shards) > 0:
        values = levels(rng, extent, shards, -0.22, 0.18) * values
    return jnp.clip(values, min=-reach, max=reach).astype(kind)


def setup_inputs(seed: int = 0, part: int = 0) -> dict:
    splits = jax.random.split(jax.random.key(seed), 5)
    part_splits = jax.random.split(jax.random.fold_in(splits[4], part), 5)
    fractions = jnp.clip(1.0 * jax.random.uniform(part_splits[0], (3, ELEC), jnp.float32) ** levels(part_splits[0], (3, ELEC), ((1, 16),), -0.2, 0.2), 0.0, 1.0)
    cell_index = place_ends(jax.random.randint(part_splits[1], (2, ELEC), 0, GW), jax.random.fold_in(part_splits[1], 1), 0, GW - 1).astype(jnp.int32)
    slab_owner_keys = jax.random.split(jax.random.fold_in(part_splits[2], 1), ELEC // E_DEV)
    slab_owner_turns = jax.random.permutation(jax.random.fold_in(part_splits[2], 3), ELEC // E_DEV)
    slab_owner = jax.vmap(lambda own, number: shared_out(jax.random.fold_in(part_splits[2], 2), own, number, E_DEV, N_SLAB, 1, CAPO, 2))(slab_owner_keys, slab_owner_turns).reshape((ELEC, 1))
    spline_table = normal_values(splits[3], (N_SLAB, GW, GW, 4, ORBS), 1.0, 6.0, ((0, 4), (4, 4)), jnp.float32)
    return dict(fractions=fractions, cell_index=cell_index, slab_owner=slab_owner, spline_table=spline_table)


def spline_bases(position):
    remain = 1.0 - position
    square = position * position
    frac_cube = square * position
    values = jnp.stack([remain * remain * remain / 6.0, (3.0 * frac_cube - 6.0 * square + 4.0) / 6.0, (-3.0 * frac_cube + 3.0 * square + 3.0 * position + 1.0) / 6.0, frac_cube / 6.0], axis=-1)
    slopes = jnp.stack([-0.5 * remain * remain, 0.5 * (3.0 * square - 4.0 * position), 0.5 * (-3.0 * square + 2.0 * position + 1.0), 0.5 * square], axis=-1)
    curves = jnp.stack([remain, 3.0 * position - 2.0, 1.0 - 3.0 * position, position], axis=-1)
    return values, slopes, curves


def outer_weight(along_x, along_y, along_z):
    return along_x[:, None, None, :] * along_y[:, :, None, None] * along_z[:, None, :, None]


def reference(fractions, cell_index, slab_owner, spline_table):
    block_rows = 128
    electrons = slab_owner.shape[0]
    blocks = electrons // block_rows
    grid_width = spline_table.shape[1]
    offsets = jnp.arange(4, dtype=jnp.int32)

    def evaluate(block_index):
        first_row = (block_index * block_rows).astype(jnp.int32)
        part_frac = lax.dynamic_slice_in_dim(fractions, first_row, block_rows, 1)
        part_cells = lax.dynamic_slice_in_dim(cell_index, first_row, block_rows, 1)
        part_owner = lax.dynamic_slice_in_dim(slab_owner, first_row, block_rows, 0)[:, 0]
        basis_x, slope_x, curve_x = spline_bases(part_frac[0])
        basis_y, slope_y, curve_y = spline_bases(part_frac[1])
        basis_z, slope_z, curve_z = spline_bases(part_frac[2])
        rows_y = (part_cells[0][:, None] + offsets[None, :]) % grid_width
        rows_z = (part_cells[1][:, None] + offsets[None, :]) % grid_width
        coefficients = spline_table[part_owner[:, None, None], rows_y[:, :, None], rows_z[:, None, :]]
        weights = jnp.stack([
            outer_weight(basis_x, basis_y, basis_z),
            outer_weight(slope_x, basis_y, basis_z),
            outer_weight(basis_x, slope_y, basis_z),
            outer_weight(basis_x, basis_y, slope_z),
            outer_weight(curve_x, basis_y, basis_z) + outer_weight(basis_x, curve_y, basis_z) + outer_weight(basis_x, basis_y, curve_z),
        ])
        result = jnp.einsum("kbyza,byzao->kbo", weights, coefficients, precision=lax.Precision.HIGHEST)
        return result.astype(jnp.bfloat16)

    stacked = lax.map(evaluate, jnp.arange(blocks, dtype=jnp.int32))
    return jnp.transpose(stacked, (1, 0, 2, 3)).reshape(5, electrons, stacked.shape[3])
```

```python
import functools

import jax
import jax.numpy as jnp
from jax import lax
from jax.experimental import pallas as pl
from jax.experimental.pallas import tpu as pltpu
from jax.sharding import PartitionSpec as P

LANES = 128
F32 = jnp.float32
BF16 = jnp.bfloat16


def spline_taps(position):
    remain = 1.0 - position
    square = position * position
    frac_cube = square * position
    values = (
        remain * remain * remain / 6.0,
        (3.0 * frac_cube - 6.0 * square + 4.0) / 6.0,
        (-3.0 * frac_cube + 3.0 * square + 3.0 * position + 1.0) / 6.0,
        frac_cube / 6.0,
    )
    slopes = (
        -0.5 * remain * remain,
        0.5 * (3.0 * square - 4.0 * position),
        0.5 * (-3.0 * square + 2.0 * position + 1.0),
        0.5 * square,
    )
    curves = (remain, 3.0 * position - 2.0, 1.0 - 3.0 * position, position)
    return values, slopes, curves


def spline_bases(position):
    return tuple(jnp.stack(taps, axis=-1) for taps in spline_taps(position))


def spread_taps(first_cell, taps, grid_width):
    offsets = jnp.arange(4, dtype=jnp.int32)
    cells = jnp.arange(grid_width, dtype=jnp.int32)
    wrapped = (first_cell[:, None] + offsets[None, :]) % grid_width
    hits = (wrapped[:, :, None] == cells[None, None, :]).astype(jnp.float32)
    return jnp.sum(hits * taps[:, :, None], axis=1)


def evaluate(incoming, table_flat, grid_width):
    basis_x, slope_x, curve_x = spline_bases(incoming[0])
    basis_y, slope_y, curve_y = spline_bases(incoming[1])
    basis_z, slope_z, curve_z = spline_bases(incoming[2])
    row_y = incoming[3].astype(jnp.int32)
    row_z = incoming[4].astype(jnp.int32)
    value_y = spread_taps(row_y, basis_y, grid_width)[:, :, None, None]
    deriv_y = spread_taps(row_y, slope_y, grid_width)[:, :, None, None]
    second_y = spread_taps(row_y, curve_y, grid_width)[:, :, None, None]
    value_z = spread_taps(row_z, basis_z, grid_width)[:, None, :, None]
    deriv_z = spread_taps(row_z, slope_z, grid_width)[:, None, :, None]
    second_z = spread_taps(row_z, curve_z, grid_width)[:, None, :, None]
    value_x = basis_x[:, None, None, :]
    deriv_x = slope_x[:, None, None, :]
    second_x = curve_x[:, None, None, :]
    dense = jnp.stack(
        [
            value_x * value_y * value_z,
            deriv_x * value_y * value_z,
            value_x * deriv_y * value_z,
            value_x * value_y * deriv_z,
            second_x * value_y * value_z
            + value_x * second_y * value_z
            + value_x * value_y * second_z,
        ]
    )
    slot_count = incoming.shape[1]
    dense = dense.reshape(5 * slot_count, table_flat.shape[0])
    result = jnp.dot(
        dense, table_flat, precision=lax.Precision.HIGHEST, preferred_element_type=jnp.float32
    )
    return result.reshape(5, slot_count, table_flat.shape[1]).astype(jnp.bfloat16)


def slot_capacity(electrons, slab_count):
    return max(2, (5 * electrons + 4 * slab_count - 1) // (4 * slab_count))


def general_body(fractions, cell_index, slab_owner, spline_table):
    slab_count = lax.axis_size("slab")
    orb_count = lax.axis_size("orb")
    electrons = slab_owner.shape[0]
    capacity = slot_capacity(electrons, slab_count)
    grid_width = spline_table.shape[1]
    orb_local = spline_table.shape[4]
    owners = slab_owner[:, 0]
    columns = jnp.arange(slab_count, dtype=jnp.int32)
    member = (owners[:, None] == columns[None, :]).astype(jnp.int32)
    earlier = jnp.cumsum(member, axis=0) - member
    slot_place = owners * capacity + jnp.sum(earlier * member, axis=1)
    packed = jnp.concatenate([fractions, cell_index.astype(jnp.float32)], axis=0)
    outgoing = jnp.zeros((5, slab_count * capacity), jnp.float32).at[:, slot_place].set(packed)
    outgoing = outgoing.reshape(5, 1, slab_count, capacity)
    spread = lax.all_gather(outgoing, "orb", axis=1, tiled=True)
    arrived = lax.all_to_all(spread, "slab", split_axis=2, concat_axis=2, tiled=True)
    table_flat = spline_table.reshape(grid_width * grid_width * 4, orb_local)
    per_source = jnp.moveaxis(arrived.reshape(5, orb_count, slab_count * capacity), 1, 0)
    blocks = lax.map(lambda incoming: evaluate(incoming, table_flat, grid_width), per_source)
    results = jnp.moveaxis(blocks, 0, 1).reshape(5, orb_count, slab_count, capacity, orb_local)
    returned = lax.all_to_all(results, "slab", split_axis=2, concat_axis=2, tiled=True)
    at_home = lax.all_to_all(returned, "orb", split_axis=1, concat_axis=4, tiled=True)
    flat_home = at_home.reshape(5, slab_count * capacity, at_home.shape[4])
    return jnp.take(flat_home, slot_place, axis=1)


def iota(shape, dim):
    return lax.broadcasted_iota(jnp.int32, shape, dim)


def to_column(row):
    count = row.shape[1]
    spread = jnp.broadcast_to(row, (count, count))
    return jnp.sum(jnp.where(iota((count, count), 0) == iota((count, count), 1), spread, 0.0), axis=1, keepdims=True)


def pack_kernel(fractions_ref, cells_ref, owner_ref, packed_ref):
    electrons = fractions_ref.shape[1]
    owner = owner_ref[...].astype(F32)
    same = to_column(owner) == owner
    before = iota((electrons, electrons), 0) < iota((electrons, electrons), 1)
    slot = jnp.sum(jnp.where(same & before, 1.0, 0.0), axis=0, keepdims=True)
    packed_ref[...] = jnp.full(packed_ref.shape, -1.0, F32)
    packed_ref[0:3, :electrons] = fractions_ref[...]
    packed_ref[3:5, :electrons] = cells_ref[...].astype(F32)
    packed_ref[5:6, :electrons] = owner
    packed_ref[6:7, :electrons] = slot


def split_kernel(table_ref, high_ref, low_ref):
    table = table_ref[...]
    high = table.astype(BF16)
    high_ref[...] = high
    low_ref[...] = (table - high.astype(F32)).astype(BF16)


def slot_weights(home, slab, slots, grid_width, high_ref, low_ref):
    owner, slot = home[5:6, :], home[6:7, :]
    wanted = jnp.where(owner == slab.astype(F32), slot, -1.0)
    chosen = iota((slots, LANES), 0).astype(F32) == wanted
    lane = iota((slots, LANES), 1)

    def field(index):
        picked = jnp.sum(jnp.where(chosen, home[index : index + 1, :], 0.0), axis=1, keepdims=True)
        return jnp.broadcast_to(picked, (slots, LANES))

    taps_x, taps_y, taps_z = (spline_taps(field(dim)) for dim in range(3))
    first_y, first_z = field(3).astype(jnp.int32), field(4).astype(jnp.int32)
    along_x = lane & 3
    is_x = [along_x == tap for tap in range(3)]

    def pick_x(taps):
        return jnp.where(is_x[0], taps[0], jnp.where(is_x[1], taps[1], jnp.where(is_x[2], taps[2], taps[3])))

    def pick(hits, taps):
        out = jnp.where(hits[3], taps[3], 0.0)
        for tap in (2, 1, 0):
            out = jnp.where(hits[tap], taps[tap], out)
        return out

    x_value, x_slope, x_curve = (pick_x(taps) for taps in taps_x)
    offset_z = ((lane // 4) - first_z) & (grid_width - 1)
    hits_z = [offset_z == tap for tap in range(4)]
    z_value, z_slope, z_curve = (pick(hits_z, taps) for taps in taps_z)
    plain = z_value * x_value
    with_x = z_value * x_slope
    with_z = z_slope * x_value
    with_both = z_value * x_curve + z_curve * x_value
    per_chunk = LANES // (4 * grid_width)
    for chunk in range(grid_width // per_chunk):
        offset_y = (chunk * per_chunk + lane // (4 * grid_width) - first_y) & (grid_width - 1)
        hits_y = [offset_y == tap for tap in range(4)]
        y_value, y_slope, y_curve = (pick(hits_y, taps) for taps in taps_y)
        weights = (
            y_value * plain,
            y_value * with_x,
            y_slope * plain,
            y_value * with_z,
            y_value * with_both + y_curve * plain,
        )
        columns = slice(chunk * LANES, (chunk + 1) * LANES)
        for k, weight in enumerate(weights):
            high = weight.astype(BF16)
            high_ref[k * slots : (k + 1) * slots, columns] = high
            low_ref[k * slots : (k + 1) * slots, columns] = (weight - high.astype(F32)).astype(BF16)


def contract(weight_high, weight_low, table_high, table_low):
    dot = functools.partial(jnp.dot, preferred_element_type=F32)
    return dot(weight_high, table_high) + (dot(weight_low, table_high) + dot(weight_high, table_low))


def store_slots(out_ref, lanes, result, capacity, slots):
    for k in range(5):
        out_ref[k * capacity : k * capacity + slots, lanes] = result[k * slots : (k + 1) * slots].astype(BF16)


def far_kernel(capacity, slots, grid_width, skip, *refs):
    homes_refs, (high_ref, low_ref), outs, scratch = refs[:2], refs[2:4], refs[4:-4], refs[-4:]
    slab, orb = lax.axis_index("slab"), lax.axis_index("orb")
    lanes = slice(skip, high_ref.shape[1])
    for index, out_ref in enumerate(outs):
        weights = scratch[2 * (index % 2) : 2 * (index % 2) + 2]
        home = homes_refs[index // 4][orb ^ (index % 4)]
        slot_weights(home, slab, slots, grid_width, *weights)
        result = contract(weights[0][...], weights[1][...], high_ref[:, lanes], low_ref[:, lanes])
        store_slots(out_ref, slice(None), result, capacity, slots)


def near_kernel(capacity, slots, grid_width, *refs):
    homes_refs, (high_ref, low_ref), (mine_ref, other_ref) = refs[:2], refs[2:4], refs[4:6]
    outs, scratch, (far_high, far_low) = refs[6:-6], refs[-6:-2], refs[-2:]
    slab, orb, group = lax.axis_index("slab"), lax.axis_index("orb"), lax.axis_index("groups")
    half = mine_ref.shape[0]
    width = high_ref.shape[1]
    for part_ref, part in ((mine_ref, group), (other_ref, 1 - group)):
        table = part_ref[...]
        high = table.astype(BF16)
        rows = pl.ds(pl.multiple_of(part * half, half), half)
        far_high[rows, :] = high
        far_low[rows, :] = (table - high.astype(F32)).astype(BF16)
    for index, out_ref in enumerate(outs):
        home = homes_refs[index // 4][orb ^ (index % 4)]
        weights = scratch[:2]
        slot_weights(home, slab, slots, grid_width, *weights)
        result = contract(weights[0][...], weights[1][...], high_ref[...], low_ref[...])
        store_slots(out_ref, slice(0, width), result, capacity, slots)
        weights = scratch[2:]
        slot_weights(home, slab ^ 2, slots, grid_width, *weights)
        result = contract(weights[0][...], weights[1][...], far_high[...], far_low[...])
        store_slots(out_ref, slice(width, out_ref.shape[1]), result, capacity, slots)


def place_kernel(capacity, skip, packed_ref, *refs):
    near, far, out_ref = refs[:8], refs[8:16], refs[16]
    slab, orb = lax.axis_index("slab"), lax.axis_index("orb")
    electrons = out_ref.shape[1]
    rows, width = near[0].shape[0], near[0].shape[1] - skip
    owner = to_column(packed_ref[5:6, :electrons])
    slot = to_column(packed_ref[6:7, :electrons])
    column = iota((electrons, rows), 1).astype(F32)
    picks = []
    for step in range(4):
        wanted = jnp.where(owner == (slab ^ step).astype(F32), slot, -1000.0)
        picks.append(jnp.concatenate([(column == wanted + float(k * capacity)).astype(BF16) for k in range(5)], axis=0))
    dot = functools.partial(jnp.dot, preferred_element_type=F32)
    for turn in range(4):
        start = (orb ^ turn) * width
        here, beside = near[turn], near[4 + turn]
        main = dot(picks[0], here[:, skip:width]) + dot(picks[1], beside[:, skip:width])
        main = main + dot(picks[2], far[turn][...]) + dot(picks[3], far[4 + turn][...])
        edge = dot(picks[0], here[:, :skip]) + dot(picks[1], beside[:, :skip])
        edge = edge + dot(picks[2], here[:, width:]) + dot(picks[3], beside[:, width:])
        for k in range(5):
            band = slice(k * electrons, (k + 1) * electrons)
            out_ref[k, :, pl.ds(pl.multiple_of(start, LANES), skip)] = edge[band].astype(BF16)
            out_ref[k, :, pl.ds(pl.multiple_of(start + skip, LANES), width - skip)] = main[band].astype(BF16)


def swap(array, step, count, axes):
    return lax.ppermute(array, axes, [(i, i ^ step) for i in range(count)])


def small_body(fractions, cell_index, slab_owner, spline_table):
    electrons = slab_owner.shape[0]
    grid_width, orb_local = spline_table.shape[1], spline_table.shape[4]
    capacity = slot_capacity(electrons, 4)
    slots = -(-capacity // 16) * 16
    rows = 4 * capacity + slots
    taps = grid_width * grid_width * 4
    skip = orb_local // 4
    vmem = pltpu.CompilerParams(vmem_limit_bytes=48 * 1024 * 1024)

    group = lax.axis_index("groups")
    part = lax.dynamic_slice_in_dim(spline_table, group * (grid_width // 2), grid_width // 2, axis=1)
    part = part[..., :skip].reshape(taps // 2, skip)
    mine = swap(part, 2, 4, "slab")
    other = swap(mine, 1, 2, "groups")

    packed = pl.pallas_call(
        pack_kernel, out_shape=jax.ShapeDtypeStruct((8, LANES), F32), name="pack"
    )(fractions, cell_index, slab_owner.reshape(1, electrons))
    homes = [lax.all_gather(packed, "orb")]
    homes += [swap(homes[0], step, 4, "slab") for step in (1, 2, 3)]

    table_high, table_low = pl.pallas_call(
        split_kernel,
        out_shape=[jax.ShapeDtypeStruct((taps, orb_local), BF16)] * 2,
        compiler_params=vmem,
        name="split",
    )(spline_table.reshape(taps, orb_local))

    weights = [pltpu.VMEM((5 * slots, taps), BF16)] * 4
    far_out = pl.pallas_call(
        functools.partial(far_kernel, capacity, slots, grid_width, skip),
        out_shape=[jax.ShapeDtypeStruct((rows, orb_local - skip), BF16)] * 8,
        scratch_shapes=weights,
        compiler_params=vmem,
        name="far",
    )(homes[2], homes[3], table_high, table_low)
    far = [swap(block, 8 + index, 16, ("slab", "orb")) for index, block in enumerate(far_out)]
    near_out = pl.pallas_call(
        functools.partial(near_kernel, capacity, slots, grid_width),
        out_shape=[jax.ShapeDtypeStruct((rows, orb_local + skip), BF16)] * 8,
        scratch_shapes=weights + [pltpu.VMEM((taps, skip), BF16)] * 2,
        compiler_params=vmem,
        name="near",
    )(homes[0], homes[1], table_high, table_low, mine, other)
    near = [near_out[0]] + [swap(block, index, 16, ("slab", "orb")) for index, block in enumerate(near_out) if index]
    return pl.pallas_call(
        functools.partial(place_kernel, capacity, skip),
        out_shape=jax.ShapeDtypeStruct((5, electrons, 4 * orb_local), BF16),
        compiler_params=vmem,
        name="place",
    )(packed, *near, *far)


def solution(mesh):
    in_specs = (
        P(None, ("groups", "slab", "orb")),
        P(None, ("groups", "slab", "orb")),
        P(("groups", "slab", "orb"), None),
        P("slab", None, None, None, "orb"),
    )
    out_specs = P(None, ("groups", "slab", "orb"), None)
    small = (mesh.shape["groups"], mesh.shape["slab"], mesh.shape["orb"]) == (2, 4, 4)
    body = small_body if small else general_body
    return jax.shard_map(body, mesh=mesh, in_specs=in_specs, out_specs=out_specs, check_vma=False)
```

```python
import functools

import jax
import jax.numpy as jnp
from jax import lax
from jax.experimental import pallas as pl
from jax.experimental.pallas import tpu as pltpu
from jax.sharding import PartitionSpec as P

LANES = 128
F32 = jnp.float32
BF16 = jnp.bfloat16


def spline_taps(position):
    remain = 1.0 - position
    square = position * position
    frac_cube = square * position
    values = (
        remain * remain * remain / 6.0,
        (3.0 * frac_cube - 6.0 * square + 4.0) / 6.0,
        (-3.0 * frac_cube + 3.0 * square + 3.0 * position + 1.0) / 6.0,
        frac_cube / 6.0,
    )
    slopes = (
        -0.5 * remain * remain,
        0.5 * (3.0 * square - 4.0 * position),
        0.5 * (-3.0 * square + 2.0 * position + 1.0),
        0.5 * square,
    )
    curves = (remain, 3.0 * position - 2.0, 1.0 - 3.0 * position, position)
    return values, slopes, curves


def spline_bases(position):
    return tuple(jnp.stack(taps, axis=-1) for taps in spline_taps(position))


def spread_taps(first_cell, taps, grid_width):
    offsets = jnp.arange(4, dtype=jnp.int32)
    cells = jnp.arange(grid_width, dtype=jnp.int32)
    wrapped = (first_cell[:, None] + offsets[None, :]) % grid_width
    hits = (wrapped[:, :, None] == cells[None, None, :]).astype(jnp.float32)
    return jnp.sum(hits * taps[:, :, None], axis=1)


def evaluate(incoming, table_flat, grid_width):
    basis_x, slope_x, curve_x = spline_bases(incoming[0])
    basis_y, slope_y, curve_y = spline_bases(incoming[1])
    basis_z, slope_z, curve_z = spline_bases(incoming[2])
    row_y = incoming[3].astype(jnp.int32)
    row_z = incoming[4].astype(jnp.int32)
    value_y = spread_taps(row_y, basis_y, grid_width)[:, :, None, None]
    deriv_y = spread_taps(row_y, slope_y, grid_width)[:, :, None, None]
    second_y = spread_taps(row_y, curve_y, grid_width)[:, :, None, None]
    value_z = spread_taps(row_z, basis_z, grid_width)[:, None, :, None]
    deriv_z = spread_taps(row_z, slope_z, grid_width)[:, None, :, None]
    second_z = spread_taps(row_z, curve_z, grid_width)[:, None, :, None]
    value_x = basis_x[:, None, None, :]
    deriv_x = slope_x[:, None, None, :]
    second_x = curve_x[:, None, None, :]
    dense = jnp.stack(
        [
            value_x * value_y * value_z,
            deriv_x * value_y * value_z,
            value_x * deriv_y * value_z,
            value_x * value_y * deriv_z,
            second_x * value_y * value_z
            + value_x * second_y * value_z
            + value_x * value_y * second_z,
        ]
    )
    slot_count = incoming.shape[1]
    dense = dense.reshape(5 * slot_count, table_flat.shape[0])
    result = jnp.dot(
        dense, table_flat, precision=lax.Precision.HIGHEST, preferred_element_type=jnp.float32
    )
    return result.reshape(5, slot_count, table_flat.shape[1]).astype(jnp.bfloat16)


def slot_capacity(electrons, slab_count):
    return max(2, (5 * electrons + 4 * slab_count - 1) // (4 * slab_count))


def general_body(fractions, cell_index, slab_owner, spline_table):
    slab_count = lax.axis_size("slab")
    orb_count = lax.axis_size("orb")
    electrons = slab_owner.shape[0]
    capacity = slot_capacity(electrons, slab_count)
    grid_width = spline_table.shape[1]
    orb_local = spline_table.shape[4]
    owners = slab_owner[:, 0]
    columns = jnp.arange(slab_count, dtype=jnp.int32)
    member = (owners[:, None] == columns[None, :]).astype(jnp.int32)
    earlier = jnp.cumsum(member, axis=0) - member
    slot_place = owners * capacity + jnp.sum(earlier * member, axis=1)
    packed = jnp.concatenate([fractions, cell_index.astype(jnp.float32)], axis=0)
    outgoing = jnp.zeros((5, slab_count * capacity), jnp.float32).at[:, slot_place].set(packed)
    outgoing = outgoing.reshape(5, 1, slab_count, capacity)
    spread = lax.all_gather(outgoing, "orb", axis=1, tiled=True)
    arrived = lax.all_to_all(spread, "slab", split_axis=2, concat_axis=2, tiled=True)
    table_flat = spline_table.reshape(grid_width * grid_width * 4, orb_local)
    per_source = jnp.moveaxis(arrived.reshape(5, orb_count, slab_count * capacity), 1, 0)
    blocks = lax.map(lambda incoming: evaluate(incoming, table_flat, grid_width), per_source)
    results = jnp.moveaxis(blocks, 0, 1).reshape(5, orb_count, slab_count, capacity, orb_local)
    returned = lax.all_to_all(results, "slab", split_axis=2, concat_axis=2, tiled=True)
    at_home = lax.all_to_all(returned, "orb", split_axis=1, concat_axis=4, tiled=True)
    flat_home = at_home.reshape(5, slab_count * capacity, at_home.shape[4])
    return jnp.take(flat_home, slot_place, axis=1)


def iota(shape, dim):
    return lax.broadcasted_iota(jnp.int32, shape, dim)


def to_column(row):
    count = row.shape[1]
    spread = jnp.broadcast_to(row, (count, count))
    return jnp.sum(jnp.where(iota((count, count), 0) == iota((count, count), 1), spread, 0.0), axis=1, keepdims=True)


def pack_kernel(fractions_ref, cells_ref, owner_ref, packed_ref):
    electrons = fractions_ref.shape[1]
    owner = owner_ref[...].astype(F32)
    same = to_column(owner) == owner
    before = iota((electrons, electrons), 0) < iota((electrons, electrons), 1)
    slot = jnp.sum(jnp.where(same & before, 1.0, 0.0), axis=0, keepdims=True)
    packed_ref[...] = jnp.full(packed_ref.shape, -1.0, F32)
    packed_ref[0:3, :electrons] = fractions_ref[...]
    packed_ref[3:5, :electrons] = cells_ref[...].astype(F32)
    packed_ref[5:6, :electrons] = owner
    packed_ref[6:7, :electrons] = slot


def split_kernel(own_ref, partner_ref, high_ref, low_ref):
    width = own_ref.shape[1]
    for index, table_ref in enumerate((own_ref, partner_ref)):
        lanes = slice(index * width, (index + 1) * width)
        table = table_ref[...]
        high = table.astype(BF16)
        high_ref[:, lanes] = high
        low_ref[:, lanes] = (table - high.astype(F32)).astype(BF16)


def slot_weights(home, slab, slots, grid_width, high_ref, low_ref):
    owner, slot = home[5:6, :], home[6:7, :]
    wanted = jnp.where(owner == slab.astype(F32), slot, -1.0)
    chosen = iota((slots, LANES), 0).astype(F32) == wanted
    lane = iota((slots, LANES), 1)

    def field(index):
        picked = jnp.sum(jnp.where(chosen, home[index : index + 1, :], 0.0), axis=1, keepdims=True)
        return jnp.broadcast_to(picked, (slots, LANES))

    taps_x, taps_y, taps_z = (spline_taps(field(dim)) for dim in range(3))
    first_y, first_z = field(3).astype(jnp.int32), field(4).astype(jnp.int32)
    along_x = lane & 3
    is_x = [along_x == tap for tap in range(3)]

    def pick_x(taps):
        return jnp.where(is_x[0], taps[0], jnp.where(is_x[1], taps[1], jnp.where(is_x[2], taps[2], taps[3])))

    def pick(hits, taps):
        out = jnp.where(hits[3], taps[3], 0.0)
        for tap in (2, 1, 0):
            out = jnp.where(hits[tap], taps[tap], out)
        return out

    x_value, x_slope, x_curve = (pick_x(taps) for taps in taps_x)
    offset_z = ((lane // 4) - first_z) & (grid_width - 1)
    hits_z = [offset_z == tap for tap in range(4)]
    z_value, z_slope, z_curve = (pick(hits_z, taps) for taps in taps_z)
    plain = z_value * x_value
    with_x = z_value * x_slope
    with_z = z_slope * x_value
    with_both = z_value * x_curve + z_curve * x_value
    per_chunk = LANES // (4 * grid_width)
    for chunk in range(grid_width // per_chunk):
        offset_y = (chunk * per_chunk + lane // (4 * grid_width) - first_y) & (grid_width - 1)
        hits_y = [offset_y == tap for tap in range(4)]
        y_value, y_slope, y_curve = (pick(hits_y, taps) for taps in taps_y)
        weights = (
            y_value * plain,
            y_value * with_x,
            y_slope * plain,
            y_value * with_z,
            y_value * with_both + y_curve * plain,
        )
        columns = slice(chunk * LANES, (chunk + 1) * LANES)
        for k, weight in enumerate(weights):
            high = weight.astype(BF16)
            high_ref[k * slots : (k + 1) * slots, columns] = high
            low_ref[k * slots : (k + 1) * slots, columns] = (weight - high.astype(F32)).astype(BF16)


def contract(weight_high, weight_low, table_high, table_low):
    dot = functools.partial(jnp.dot, preferred_element_type=F32)
    return dot(weight_high, table_high) + (dot(weight_low, table_high) + dot(weight_high, table_low))


def store_slots(out_ref, lanes, result, capacity, slots):
    for k in range(5):
        out_ref[k * capacity : k * capacity + slots, lanes] = result[k * slots : (k + 1) * slots].astype(BF16)


def store_slots(out_ref, place, lanes, result, capacity, slots):
    for k in range(5):
        out_ref[place, k * capacity : k * capacity + slots, lanes] = result[k * slots : (k + 1) * slots].astype(BF16)


def far_kernel(capacity, slots, grid_width, skip, homes_ref, high_ref, low_ref, *refs):
    outs, scratch = refs[:2], refs[2:]
    slab = lax.axis_index("slab")
    width = high_ref.shape[1] // 2
    for index, out_ref in enumerate(outs):
        weights = scratch[2 * index : 2 * index + 2]
        slot_weights(homes_ref[index], slab, slots, grid_width, *weights)
        for half in range(2):
            lanes = slice(half * width + skip, (half + 1) * width)
            result = contract(weights[0][...], weights[1][...], high_ref[:, lanes], low_ref[:, lanes])
            place = slice(half * (width - skip), (half + 1) * (width - skip))
            for k in range(5):
                band = result[k * slots : (k + 1) * slots].astype(BF16)
                out_ref[k * capacity : k * capacity + slots, place] = band


def near_kernel(capacity, slots, grid_width, home_ref, beside_ref, high_ref, low_ref, out_ref, *scratch):
    slab, orb = lax.axis_index("slab"), lax.axis_index("orb")
    me = 2 * (slab & 1) + orb // 2
    for step in range(4):
        weights = scratch[2 * (step % 2) : 2 * (step % 2) + 2]
        home = (home_ref, beside_ref)[step // 2][step % 2]
        slot_weights(home, slab, slots, grid_width, *weights)
        result = contract(weights[0][...], weights[1][...], high_ref[...], low_ref[...])
        store_slots(out_ref, me ^ step, slice(None), result, capacity, slots)


def copied_kernel(capacity, slots, grid_width, home_ref, beside_ref, *refs):
    parts, out_ref, scratch, (high_ref, low_ref) = refs[:4], refs[4], refs[5:9], refs[9:]
    slab, orb, group = lax.axis_index("slab"), lax.axis_index("orb"), lax.axis_index("groups")
    me = 2 * (slab & 1) + orb // 2
    half, width = parts[0].shape
    for index, part_ref in enumerate(parts):
        source = group if index % 2 == 0 else 1 - group
        lanes = slice((index // 2) * width, (index // 2 + 1) * width)
        rows = pl.ds(pl.multiple_of(source * half, half), half)
        table = part_ref[...]
        high = table.astype(BF16)
        high_ref[rows, lanes] = high
        low_ref[rows, lanes] = (table - high.astype(F32)).astype(BF16)
    for step in range(4):
        weights = scratch[2 * (step % 2) : 2 * (step % 2) + 2]
        home = (home_ref, beside_ref)[step // 2][step % 2]
        slot_weights(home, slab ^ 2, slots, grid_width, *weights)
        result = contract(weights[0][...], weights[1][...], high_ref[...], low_ref[...])
        store_slots(out_ref, me ^ step, slice(None), result, capacity, slots)


def place_kernel(capacity, slots, skip, packed_ref, near_ref, copied_ref, *refs):
    far, out_ref = refs[:4], refs[4]
    slab, orb = lax.axis_index("slab"), lax.axis_index("orb")
    me = 2 * (slab & 1) + orb // 2
    electrons = out_ref.shape[1]
    width = near_ref.shape[2] // 2
    owner = to_column(packed_ref[5:6, :electrons])
    slot = to_column(packed_ref[6:7, :electrons])
    step = jnp.zeros_like(owner)
    for index in range(1, 4):
        step = jnp.where(owner == (slab ^ index).astype(F32), float(index), step)
    pick = (iota((electrons, 4 * slots), 1).astype(F32) == step * float(slots) + slot).astype(BF16)
    for turn in range(2):
        here, beside = me ^ turn, me ^ (2 + turn)
        for half in range(2):
            start = (orb ^ (2 * turn + half)) * width
            for k in range(5):
                rows = slice(k * capacity, k * capacity + slots)
                main = slice(half * width + skip, (half + 1) * width)
                main_far = slice(half * (width - skip), (half + 1) * (width - skip))
                edge = slice(half * width, half * width + skip)
                edge_far = slice(half * skip, (half + 1) * skip)
                blocks = [near_ref[here, rows, main], near_ref[beside, rows, main], far[turn][rows, main_far], far[2 + turn][rows, main_far]]
                placed = jnp.dot(pick, jnp.concatenate(blocks, axis=0), preferred_element_type=F32)
                out_ref[k, :, pl.ds(pl.multiple_of(start + skip, LANES), width - skip)] = placed.astype(BF16)
                blocks = [near_ref[here, rows, edge], near_ref[beside, rows, edge], copied_ref[here, rows, edge_far], copied_ref[beside, rows, edge_far]]
                placed = jnp.dot(pick, jnp.concatenate(blocks, axis=0), preferred_element_type=F32)
                out_ref[k, :, pl.ds(pl.multiple_of(start, LANES), skip)] = placed.astype(BF16)


def swap(array, step, count, axes):
    return lax.ppermute(array, axes, [(i, i ^ step) for i in range(count)])


def after(array, *others):
    return lax.optimization_barrier((array, *others))[0]


def trade(blocks):
    members = [[4 * (2 * pair + s) + 2 * x + core for s in range(2) for x in range(2)] for pair in range(2) for core in range(2)]
    return lax.all_to_all(blocks, ("slab", "orb"), 0, 0, axis_index_groups=members, tiled=True)


def small_body(fractions, cell_index, slab_owner, spline_table):
    electrons = slab_owner.shape[0]
    grid_width, orb_local = spline_table.shape[1], spline_table.shape[4]
    capacity = slot_capacity(electrons, 4)
    slots = -(-capacity // 16) * 16
    rows = 4 * capacity + slots
    taps = grid_width * grid_width * 4
    skip = orb_local // 4
    vmem = pltpu.CompilerParams(vmem_limit_bytes=48 * 1024 * 1024)
    weights = [pltpu.VMEM((5 * slots, taps), BF16)] * 4

    partner_table = swap(spline_table, 1, 4, "orb")
    packed = pl.pallas_call(
        pack_kernel, out_shape=jax.ShapeDtypeStruct((8, LANES), F32), name="pack"
    )(fractions, cell_index, slab_owner.reshape(1, electrons))
    home = jnp.stack([packed, swap(packed, 2, 4, "orb")])
    beside, across, corner = (swap(home, step, 4, "slab") for step in (1, 2, 3))

    group = lax.axis_index("groups")
    part = lax.dynamic_slice_in_dim(after(spline_table, home), group * (grid_width // 2), grid_width // 2, axis=1)
    part = part[..., :skip].reshape(taps // 2, skip)
    mine = swap(part, 2, 4, "slab")

    table_high, table_low = pl.pallas_call(
        split_kernel,
        out_shape=[jax.ShapeDtypeStruct((taps, 2 * orb_local), BF16)] * 2,
        compiler_params=vmem,
        name="split",
    )(spline_table.reshape(taps, orb_local), partner_table.reshape(taps, orb_local))

    def far_blocks(homes):
        return pl.pallas_call(
            functools.partial(far_kernel, capacity, slots, grid_width, skip),
            out_shape=[jax.ShapeDtypeStruct((rows, 2 * (orb_local - skip)), BF16)] * 2,
            scratch_shapes=weights,
            compiler_params=vmem,
            name="far",
        )(homes, table_high, table_low)

    far_out = far_blocks(across) + far_blocks(corner)
    far = [swap(block, 8 + 2 * index, 16, ("slab", "orb")) for index, block in enumerate(far_out)]

    mine_late = after(mine, *far_out[:2])
    other = swap(mine_late, 1, 2, "groups")
    mine_partner = swap(mine_late, 1, 4, "orb")
    other_partner = swap(other, 1, 4, "orb")

    near_out = pl.pallas_call(
        functools.partial(near_kernel, capacity, slots, grid_width),
        out_shape=jax.ShapeDtypeStruct((4, rows, 2 * orb_local), BF16),
        scratch_shapes=weights,
        compiler_params=vmem,
        name="near",
    )(home, beside, table_high, table_low)
    near = trade(near_out)
    copied_out = pl.pallas_call(
        functools.partial(copied_kernel, capacity, slots, grid_width),
        out_shape=jax.ShapeDtypeStruct((4, rows, 2 * skip), BF16),
        scratch_shapes=weights + [pltpu.VMEM((taps, 2 * skip), BF16)] * 2,
        compiler_params=vmem,
        name="copied",
    )(home, beside, mine_late, other, mine_partner, other_partner)
    copied = trade(copied_out)
    return pl.pallas_call(
        functools.partial(place_kernel, capacity, slots, skip),
        out_shape=jax.ShapeDtypeStruct((5, electrons, 4 * orb_local), BF16),
        compiler_params=vmem,
        name="place",
    )(packed, near, copied, *far)


def solution(mesh):
    in_specs = (
        P(None, ("groups", "slab", "orb")),
        P(None, ("groups", "slab", "orb")),
        P(("groups", "slab", "orb"), None),
        P("slab", None, None, None, "orb"),
    )
    out_specs = P(None, ("groups", "slab", "orb"), None)
    small = (mesh.shape["groups"], mesh.shape["slab"], mesh.shape["orb"]) == (2, 4, 4)
    body = small_body if small else general_body
    return jax.shard_map(body, mesh=mesh, in_specs=in_specs, out_specs=out_specs, check_vma=False)
```

```python
import functools

import jax
import jax.numpy as jnp
from jax import lax
from jax.experimental import pallas as pl
from jax.experimental.pallas import tpu as pltpu
from jax.sharding import PartitionSpec as P

LANES = 128
F32 = jnp.float32
BF16 = jnp.bfloat16


def spline_taps(position):
    remain = 1.0 - position
    square = position * position
    frac_cube = square * position
    values = (
        remain * remain * remain / 6.0,
        (3.0 * frac_cube - 6.0 * square + 4.0) / 6.0,
        (-3.0 * frac_cube + 3.0 * square + 3.0 * position + 1.0) / 6.0,
        frac_cube / 6.0,
    )
    slopes = (
        -0.5 * remain * remain,
        0.5 * (3.0 * square - 4.0 * position),
        0.5 * (-3.0 * square + 2.0 * position + 1.0),
        0.5 * square,
    )
    curves = (remain, 3.0 * position - 2.0, 1.0 - 3.0 * position, position)
    return values, slopes, curves


def spline_bases(position):
    return tuple(jnp.stack(taps, axis=-1) for taps in spline_taps(position))


def spread_taps(first_cell, taps, grid_width):
    offsets = jnp.arange(4, dtype=jnp.int32)
    cells = jnp.arange(grid_width, dtype=jnp.int32)
    wrapped = (first_cell[:, None] + offsets[None, :]) % grid_width
    hits = (wrapped[:, :, None] == cells[None, None, :]).astype(jnp.float32)
    return jnp.sum(hits * taps[:, :, None], axis=1)


def evaluate(incoming, table_flat, grid_width):
    basis_x, slope_x, curve_x = spline_bases(incoming[0])
    basis_y, slope_y, curve_y = spline_bases(incoming[1])
    basis_z, slope_z, curve_z = spline_bases(incoming[2])
    row_y = incoming[3].astype(jnp.int32)
    row_z = incoming[4].astype(jnp.int32)
    value_y = spread_taps(row_y, basis_y, grid_width)[:, :, None, None]
    deriv_y = spread_taps(row_y, slope_y, grid_width)[:, :, None, None]
    second_y = spread_taps(row_y, curve_y, grid_width)[:, :, None, None]
    value_z = spread_taps(row_z, basis_z, grid_width)[:, None, :, None]
    deriv_z = spread_taps(row_z, slope_z, grid_width)[:, None, :, None]
    second_z = spread_taps(row_z, curve_z, grid_width)[:, None, :, None]
    value_x = basis_x[:, None, None, :]
    deriv_x = slope_x[:, None, None, :]
    second_x = curve_x[:, None, None, :]
    dense = jnp.stack(
        [
            value_x * value_y * value_z,
            deriv_x * value_y * value_z,
            value_x * deriv_y * value_z,
            value_x * value_y * deriv_z,
            second_x * value_y * value_z
            + value_x * second_y * value_z
            + value_x * value_y * second_z,
        ]
    )
    slot_count = incoming.shape[1]
    dense = dense.reshape(5 * slot_count, table_flat.shape[0])
    result = jnp.dot(
        dense, table_flat, precision=lax.Precision.HIGHEST, preferred_element_type=jnp.float32
    )
    return result.reshape(5, slot_count, table_flat.shape[1]).astype(jnp.bfloat16)


def slot_capacity(electrons, slab_count):
    return max(2, (5 * electrons + 4 * slab_count - 1) // (4 * slab_count))


def general_body(fractions, cell_index, slab_owner, spline_table):
    slab_count = lax.axis_size("slab")
    orb_count = lax.axis_size("orb")
    electrons = slab_owner.shape[0]
    capacity = slot_capacity(electrons, slab_count)
    grid_width = spline_table.shape[1]
    orb_local = spline_table.shape[4]
    owners = slab_owner[:, 0]
    columns = jnp.arange(slab_count, dtype=jnp.int32)
    member = (owners[:, None] == columns[None, :]).astype(jnp.int32)
    earlier = jnp.cumsum(member, axis=0) - member
    slot_place = owners * capacity + jnp.sum(earlier * member, axis=1)
    packed = jnp.concatenate([fractions, cell_index.astype(jnp.float32)], axis=0)
    outgoing = jnp.zeros((5, slab_count * capacity), jnp.float32).at[:, slot_place].set(packed)
    outgoing = outgoing.reshape(5, 1, slab_count, capacity)
    spread = lax.all_gather(outgoing, "orb", axis=1, tiled=True)
    arrived = lax.all_to_all(spread, "slab", split_axis=2, concat_axis=2, tiled=True)
    table_flat = spline_table.reshape(grid_width * grid_width * 4, orb_local)
    per_source = jnp.moveaxis(arrived.reshape(5, orb_count, slab_count * capacity), 1, 0)
    blocks = lax.map(lambda incoming: evaluate(incoming, table_flat, grid_width), per_source)
    results = jnp.moveaxis(blocks, 0, 1).reshape(5, orb_count, slab_count, capacity, orb_local)
    returned = lax.all_to_all(results, "slab", split_axis=2, concat_axis=2, tiled=True)
    at_home = lax.all_to_all(returned, "orb", split_axis=1, concat_axis=4, tiled=True)
    flat_home = at_home.reshape(5, slab_count * capacity, at_home.shape[4])
    return jnp.take(flat_home, slot_place, axis=1)


def iota(shape, dim):
    return lax.broadcasted_iota(jnp.int32, shape, dim)


def to_column(row):
    count = row.shape[1]
    spread = jnp.broadcast_to(row, (count, count))
    return jnp.sum(jnp.where(iota((count, count), 0) == iota((count, count), 1), spread, 0.0), axis=1, keepdims=True)


def pack_kernel(fractions_ref, cells_ref, owner_ref, packed_ref):
    electrons = fractions_ref.shape[1]
    owner = owner_ref[...].astype(F32)
    same = to_column(owner) == owner
    before = iota((electrons, electrons), 0) < iota((electrons, electrons), 1)
    slot = jnp.sum(jnp.where(same & before, 1.0, 0.0), axis=0, keepdims=True)
    packed_ref[...] = jnp.full(packed_ref.shape, -1.0, F32)
    packed_ref[0:3, :electrons] = fractions_ref[...]
    packed_ref[3:5, :electrons] = cells_ref[...].astype(F32)
    packed_ref[5:6, :electrons] = owner
    packed_ref[6:7, :electrons] = slot


def split_kernel(planes, table_ref, high_ref, low_ref):
    blocks = high_ref.shape[1] // LANES
    count = table_ref.shape[0] // (blocks * planes)
    for block in range(blocks):
        for plane in range(planes):
            table = table_ref[pl.ds(block * planes + plane, count, stride=blocks * planes), :]
            high = table.astype(BF16)
            rows, lanes = slice(plane * count, (plane + 1) * count), slice(block * LANES, (block + 1) * LANES)
            high_ref[rows, lanes] = high
            low_ref[rows, lanes] = (table - high.astype(F32)).astype(BF16)


def slot_weights(home, slab, slots, grid_width, high_ref, low_ref):
    owner, slot = home[5:6, :], home[6:7, :]
    wanted = jnp.where(owner == slab.astype(F32), slot, -1.0)
    chosen = iota((slots, LANES), 0).astype(F32) == wanted
    lane = iota((slots, LANES), 1)

    def field(index):
        picked = jnp.sum(jnp.where(chosen, home[index : index + 1, :], 0.0), axis=1, keepdims=True)
        return jnp.broadcast_to(picked, (slots, LANES))

    (x_value, x_slope, x_curve), taps_y, taps_z = (spline_taps(field(dim)) for dim in range(3))
    first_y, first_z = field(3).astype(jnp.int32), field(4).astype(jnp.int32)

    def pick(offset, kinds):
        hits = [offset == tap for tap in range(4)]
        picked = []
        for taps in kinds:
            out = jnp.where(hits[3], taps[3], 0.0)
            for tap in (2, 1, 0):
                out = jnp.where(hits[tap], taps[tap], out)
            picked.append(out)
        return picked

    z_value, z_slope, z_curve = pick(((lane & (grid_width - 1)) - first_z) & (grid_width - 1), taps_z)
    per_chunk = LANES // grid_width
    for chunk in range(grid_width // per_chunk):
        offset_y = (chunk * per_chunk + lane // grid_width - first_y) & (grid_width - 1)
        y_value, y_slope, y_curve = pick(offset_y, taps_y)
        plain = y_value * z_value
        with_y = y_slope * z_value
        with_z = y_value * z_slope
        with_both = y_curve * z_value + y_value * z_curve
        for plane in range(4):
            weights = (
                x_value[plane] * plain,
                x_slope[plane] * plain,
                x_value[plane] * with_y,
                x_value[plane] * with_z,
                x_curve[plane] * plain + x_value[plane] * with_both,
            )
            start = plane * grid_width * grid_width + chunk * LANES
            for k, weight in enumerate(weights):
                high = weight.astype(BF16)
                high_ref[k * slots : (k + 1) * slots, start : start + LANES] = high
                low_ref[k * slots : (k + 1) * slots, start : start + LANES] = (weight - high.astype(F32)).astype(BF16)


def contract(weights, table_high, table_low):
    dot = functools.partial(jnp.dot, preferred_element_type=F32)
    high, low = weights[0][...], weights[1][...]
    return dot(high, table_high) + (dot(low, table_high) + dot(high, table_low))


def store_slots(out_ref, lanes, result, capacity, slots):
    for k in range(5):
        out_ref[k * capacity : k * capacity + slots, lanes] = result[k * slots : (k + 1) * slots].astype(BF16)


def serve_kernel(sizes, tables_count, *refs):
    capacity, slots, grid_width = sizes
    tables, refs = refs[: 2 * tables_count], refs[2 * tables_count :]
    weights, sems = refs[-5:-1], refs[-1]
    count = (len(refs) - 5) * 2 // 5
    homes_refs, outs, staged = refs[: count // 2], refs[count // 2 : count // 2 + count], refs[count // 2 + count : -5]
    slab = lax.axis_index("slab")
    copies = []
    for index in range(count):
        pair = weights[2 * (index % 2) : 2 * (index % 2) + 2]
        slot_weights(homes_refs[index // 2][index % 2], slab, slots, grid_width, *pair)
        for half in range(tables_count):
            high_ref, low_ref = tables[2 * half : 2 * half + 2]
            width = high_ref.shape[1]
            result = contract(pair, high_ref[...], low_ref[...])
            store_slots(staged[index], slice(half * width, (half + 1) * width), result, capacity, slots)
        copy = pltpu.make_async_copy(staged[index], outs[index], sems.at[index])
        copy.start()
        copies.append(copy)
    for copy in copies:
        copy.wait()


def place_kernel(capacity, slots, packed_ref, *refs):
    pieces, out_ref, landed, placed, sems = refs[:8], refs[8], refs[9:17], refs[17], refs[18]
    slab, orb = lax.axis_index("slab"), lax.axis_index("orb")
    arrivals = [pltpu.make_async_copy(piece, buffer, sems.at[index]) for index, (piece, buffer) in enumerate(zip(pieces, landed))]
    for turn in range(2):
        for arrival in arrivals[turn::2]:
            arrival.start()
    electrons = out_ref.shape[1]
    width = out_ref.shape[2] // 4
    owner = to_column(packed_ref[5:6, :electrons])
    slot = to_column(packed_ref[6:7, :electrons])
    step = jnp.zeros_like(owner)
    for index in range(1, 4):
        step = jnp.where(owner == (slab ^ index).astype(F32), float(index), step)
    pick = (iota((electrons, 4 * slots), 1).astype(F32) == step * float(slots) + slot).astype(BF16)
    departures = []
    for turn in range(2):
        for arrival in arrivals[turn::2]:
            arrival.wait()
        for half in range(2):
            block = 2 * turn + half
            lanes = slice(half * width, (half + 1) * width)
            for k in range(5):
                rows = slice(k * capacity, k * capacity + slots)
                stack = jnp.concatenate([buffer[rows, lanes] for buffer in landed[turn::2]], axis=0)
                placed[block, k] = jnp.dot(pick, stack, preferred_element_type=F32).astype(BF16)
            start = pl.multiple_of((orb ^ block) * width, LANES)
            departure = pltpu.make_async_copy(placed.at[block], out_ref.at[:, :, pl.ds(start, width)], sems.at[len(pieces) + block])
            departure.start()
            departures.append(departure)
    for departure in departures:
        departure.wait()


def swap(array, step, count, axes):
    return lax.ppermute(array, axes, [(i, i ^ step) for i in range(count)])


def after(array, *others):
    return lax.optimization_barrier((array, *others))[0]


HBM = pl.BlockSpec(memory_space=pltpu.HBM)
VMEM = pl.BlockSpec(memory_space=pltpu.VMEM)


def small_body(fractions, cell_index, slab_owner, spline_table):
    electrons = slab_owner.shape[0]
    grid_width, planes, orb_local = spline_table.shape[1], spline_table.shape[3], spline_table.shape[4]
    capacity = slot_capacity(electrons, 4)
    slots = -(-capacity // 16) * 16
    rows, width = 4 * capacity + slots, 2 * orb_local
    taps = grid_width * grid_width * planes
    vmem = pltpu.CompilerParams(vmem_limit_bytes=40 * 1024 * 1024)
    blocks = functools.partial(jax.ShapeDtypeStruct, dtype=BF16)
    both_axes = ("slab", "orb")

    partner_table = swap(spline_table, 1, 4, "orb")
    packed = pl.pallas_call(
        pack_kernel, out_shape=jax.ShapeDtypeStruct((8, LANES), F32), name="pack"
    )(fractions, cell_index, slab_owner.reshape(1, electrons))
    home = jnp.stack([packed, swap(packed, 2, 4, "orb")])
    across, corner, beside = (swap(home, step, 4, "slab") for step in (2, 3, 1))

    def split(table):
        view = table.reshape(grid_width * grid_width, planes, orb_local // LANES, LANES)
        view = view.transpose(0, 2, 1, 3).reshape(taps * orb_local // LANES, LANES)
        return pl.pallas_call(
            functools.partial(split_kernel, planes),
            out_shape=[blocks((taps, orb_local))] * 2,
            compiler_params=vmem,
            name="split",
        )(view)

    tables = split(spline_table) + split(partner_table)

    def serve(name, *homes):
        count = 2 * len(homes)
        return pl.pallas_call(
            functools.partial(serve_kernel, (capacity, slots, grid_width), 2),
            out_shape=[blocks((rows, width))] * count,
            in_specs=[VMEM] * (4 + len(homes)),
            out_specs=[HBM] * count,
            scratch_shapes=[pltpu.VMEM((rows, width), BF16)] * count
            + [pltpu.VMEM((5 * slots, taps), BF16)] * 4
            + [pltpu.SemaphoreType.DMA((count,))],
            compiler_params=vmem,
            name=name,
        )(*tables, *homes)

    def send(step, block):
        return swap(block, step, 16, both_axes)

    across_out = serve("across", after(across, corner, beside))
    corner_out = serve("corner", after(corner, *across_out))
    near_out = serve("near", after(home, *corner_out), beside)
    far = [send(8 + 2 * index, block) for index, block in enumerate(across_out + corner_out)]
    near = [near_out[0]] + [send(2 * index, near_out[index]) for index in range(1, 4)]
    return pl.pallas_call(
        functools.partial(place_kernel, capacity, slots),
        out_shape=blocks((5, electrons, 4 * orb_local)),
        in_specs=[VMEM] + [HBM] * 8,
        out_specs=HBM,
        scratch_shapes=[pltpu.VMEM((rows, width), BF16)] * 8
        + [pltpu.VMEM((4, 5, electrons, orb_local), BF16), pltpu.SemaphoreType.DMA((12,))],
        compiler_params=vmem,
        name="place",
    )(packed, *near, *far)


def solution(mesh):
    in_specs = (
        P(None, ("groups", "slab", "orb")),
        P(None, ("groups", "slab", "orb")),
        P(("groups", "slab", "orb"), None),
        P("slab", None, None, None, "orb"),
    )
    out_specs = P(None, ("groups", "slab", "orb"), None)
    small = (mesh.shape["groups"], mesh.shape["slab"], mesh.shape["orb"]) == (2, 4, 4)
    body = small_body if small else general_body
    return jax.shard_map(body, mesh=mesh, in_specs=in_specs, out_specs=out_specs, check_vma=False)
```

```python
import functools

import jax
import jax.numpy as jnp
from jax import lax
from jax.experimental import pallas as pl
from jax.experimental.pallas import tpu as pltpu
from jax.sharding import PartitionSpec as P

LANES = 128
F32 = jnp.float32
BF16 = jnp.bfloat16


def spline_taps(position):
    remain = 1.0 - position
    square = position * position
    frac_cube = square * position
    values = (
        remain * remain * remain / 6.0,
        (3.0 * frac_cube - 6.0 * square + 4.0) / 6.0,
        (-3.0 * frac_cube + 3.0 * square + 3.0 * position + 1.0) / 6.0,
        frac_cube / 6.0,
    )
    slopes = (
        -0.5 * remain * remain,
        0.5 * (3.0 * square - 4.0 * position),
        0.5 * (-3.0 * square + 2.0 * position + 1.0),
        0.5 * square,
    )
    curves = (remain, 3.0 * position - 2.0, 1.0 - 3.0 * position, position)
    return values, slopes, curves


def spline_bases(position):
    return tuple(jnp.stack(taps, axis=-1) for taps in spline_taps(position))


def spread_taps(first_cell, taps, grid_width):
    offsets = jnp.arange(4, dtype=jnp.int32)
    cells = jnp.arange(grid_width, dtype=jnp.int32)
    wrapped = (first_cell[:, None] + offsets[None, :]) % grid_width
    hits = (wrapped[:, :, None] == cells[None, None, :]).astype(jnp.float32)
    return jnp.sum(hits * taps[:, :, None], axis=1)


def evaluate(incoming, table_flat, grid_width):
    basis_x, slope_x, curve_x = spline_bases(incoming[0])
    basis_y, slope_y, curve_y = spline_bases(incoming[1])
    basis_z, slope_z, curve_z = spline_bases(incoming[2])
    row_y = incoming[3].astype(jnp.int32)
    row_z = incoming[4].astype(jnp.int32)
    value_y = spread_taps(row_y, basis_y, grid_width)[:, :, None, None]
    deriv_y = spread_taps(row_y, slope_y, grid_width)[:, :, None, None]
    second_y = spread_taps(row_y, curve_y, grid_width)[:, :, None, None]
    value_z = spread_taps(row_z, basis_z, grid_width)[:, None, :, None]
    deriv_z = spread_taps(row_z, slope_z, grid_width)[:, None, :, None]
    second_z = spread_taps(row_z, curve_z, grid_width)[:, None, :, None]
    value_x = basis_x[:, None, None, :]
    deriv_x = slope_x[:, None, None, :]
    second_x = curve_x[:, None, None, :]
    dense = jnp.stack(
        [
            value_x * value_y * value_z,
            deriv_x * value_y * value_z,
            value_x * deriv_y * value_z,
            value_x * value_y * deriv_z,
            second_x * value_y * value_z
            + value_x * second_y * value_z
            + value_x * value_y * second_z,
        ]
    )
    slot_count = incoming.shape[1]
    dense = dense.reshape(5 * slot_count, table_flat.shape[0])
    result = jnp.dot(
        dense, table_flat, precision=lax.Precision.HIGHEST, preferred_element_type=jnp.float32
    )
    return result.reshape(5, slot_count, table_flat.shape[1]).astype(jnp.bfloat16)


def slot_capacity(electrons, slab_count):
    return max(2, (5 * electrons + 4 * slab_count - 1) // (4 * slab_count))


def general_body(fractions, cell_index, slab_owner, spline_table):
    slab_count = lax.axis_size("slab")
    orb_count = lax.axis_size("orb")
    electrons = slab_owner.shape[0]
    capacity = slot_capacity(electrons, slab_count)
    grid_width = spline_table.shape[1]
    orb_local = spline_table.shape[4]
    owners = slab_owner[:, 0]
    columns = jnp.arange(slab_count, dtype=jnp.int32)
    member = (owners[:, None] == columns[None, :]).astype(jnp.int32)
    earlier = jnp.cumsum(member, axis=0) - member
    slot_place = owners * capacity + jnp.sum(earlier * member, axis=1)
    packed = jnp.concatenate([fractions, cell_index.astype(jnp.float32)], axis=0)
    outgoing = jnp.zeros((5, slab_count * capacity), jnp.float32).at[:, slot_place].set(packed)
    outgoing = outgoing.reshape(5, 1, slab_count, capacity)
    spread = lax.all_gather(outgoing, "orb", axis=1, tiled=True)
    arrived = lax.all_to_all(spread, "slab", split_axis=2, concat_axis=2, tiled=True)
    table_flat = spline_table.reshape(grid_width * grid_width * 4, orb_local)
    per_source = jnp.moveaxis(arrived.reshape(5, orb_count, slab_count * capacity), 1, 0)
    blocks = lax.map(lambda incoming: evaluate(incoming, table_flat, grid_width), per_source)
    results = jnp.moveaxis(blocks, 0, 1).reshape(5, orb_count, slab_count, capacity, orb_local)
    returned = lax.all_to_all(results, "slab", split_axis=2, concat_axis=2, tiled=True)
    at_home = lax.all_to_all(returned, "orb", split_axis=1, concat_axis=4, tiled=True)
    flat_home = at_home.reshape(5, slab_count * capacity, at_home.shape[4])
    return jnp.take(flat_home, slot_place, axis=1)


def iota(shape, dim):
    return lax.broadcasted_iota(jnp.int32, shape, dim)


def to_column(row):
    count = row.shape[1]
    spread = jnp.broadcast_to(row, (count, count))
    return jnp.sum(jnp.where(iota((count, count), 0) == iota((count, count), 1), spread, 0.0), axis=1, keepdims=True)


def pack_kernel(fractions_ref, cells_ref, owner_ref, packed_ref):
    electrons = fractions_ref.shape[1]
    owner = owner_ref[...].astype(F32)
    same = to_column(owner) == owner
    before = iota((electrons, electrons), 0) < iota((electrons, electrons), 1)
    slot = jnp.sum(jnp.where(same & before, 1.0, 0.0), axis=0, keepdims=True)
    packed_ref[...] = jnp.full(packed_ref.shape, -1.0, F32)
    packed_ref[0:3, :electrons] = fractions_ref[...]
    packed_ref[3:5, :electrons] = cells_ref[...].astype(F32)
    packed_ref[5:6, :electrons] = owner
    packed_ref[6:7, :electrons] = slot


def split_kernel(planes, table_ref, high_ref, low_ref, landed, sems):
    blocks = high_ref.shape[1] // LANES
    pieces = sems.shape[0]
    piece = table_ref.shape[0] // pieces
    count = piece // (blocks * planes)
    copies = []
    for index in range(pieces):
        span = slice(index * piece, (index + 1) * piece)
        copies.append(pltpu.make_async_copy(table_ref.at[span, :], landed.at[span, :], sems.at[index]))
        copies[-1].start()
    for index in range(pieces):
        copies[index].wait()
        for block in range(blocks):
            lanes = slice(block * LANES, (block + 1) * LANES)
            for plane in range(planes):
                first = index * piece + block * planes + plane
                table = landed[pl.ds(first, count, stride=blocks * planes), :]
                high = table.astype(BF16)
                start = (plane * pieces + index) * count
                high_ref[start : start + count, lanes] = high
                low_ref[start : start + count, lanes] = (table - high.astype(F32)).astype(BF16)


def slot_weights(home, slab, slots, grid_width, high_ref, low_ref):
    owner, slot = home[5:6, :], home[6:7, :]
    wanted = jnp.where(owner == slab.astype(F32), slot, -1.0)
    chosen = iota((slots, LANES), 0).astype(F32) == wanted
    lane = iota((slots, LANES), 1)

    def field(index):
        picked = jnp.sum(jnp.where(chosen, home[index : index + 1, :], 0.0), axis=1, keepdims=True)
        return jnp.broadcast_to(picked, (slots, LANES))

    (x_value, x_slope, x_curve), taps_y, taps_z = (spline_taps(field(dim)) for dim in range(3))
    first_y, first_z = field(3).astype(jnp.int32), field(4).astype(jnp.int32)

    def pick(offset, kinds):
        hits = [offset == tap for tap in range(4)]
        picked = []
        for taps in kinds:
            out = jnp.where(hits[3], taps[3], 0.0)
            for tap in (2, 1, 0):
                out = jnp.where(hits[tap], taps[tap], out)
            picked.append(out)
        return picked

    z_value, z_slope, z_curve = pick(((lane & (grid_width - 1)) - first_z) & (grid_width - 1), taps_z)
    per_chunk = LANES // grid_width
    for chunk in range(grid_width // per_chunk):
        offset_y = (chunk * per_chunk + lane // grid_width - first_y) & (grid_width - 1)
        y_value, y_slope, y_curve = pick(offset_y, taps_y)
        plain = y_value * z_value
        with_y = y_slope * z_value
        with_z = y_value * z_slope
        with_both = y_curve * z_value + y_value * z_curve
        for plane in range(4):
            weights = (
                x_value[plane] * plain,
                x_slope[plane] * plain,
                x_value[plane] * with_y,
                x_value[plane] * with_z,
                x_curve[plane] * plain + x_value[plane] * with_both,
            )
            start = plane * grid_width * grid_width + chunk * LANES
            for k, weight in enumerate(weights):
                high = weight.astype(BF16)
                high_ref[k * slots : (k + 1) * slots, start : start + LANES] = high
                low_ref[k * slots : (k + 1) * slots, start : start + LANES] = (weight - high.astype(F32)).astype(BF16)


def contract(weights, table_high, table_low):
    dot = functools.partial(jnp.dot, preferred_element_type=F32)
    high, low = weights[0][...], weights[1][...]
    return dot(high, table_high) + (dot(low, table_high) + dot(high, table_low))


def store_slots(out_ref, lanes, result, capacity, slots):
    for k in range(5):
        out_ref[k * capacity : k * capacity + slots, lanes] = result[k * slots : (k + 1) * slots].astype(BF16)


def serve_kernel(sizes, places, *refs):
    capacity, slots, grid_width = sizes
    count = len(places)
    weights, sems = refs[-5:-1], refs[-1]
    tables, homes_refs, outs, staged = refs[:4], refs[4 : -5 - 2 * count], refs[-5 - 2 * count : -5 - count], refs[-5 - count : -5]
    slab = lax.axis_index("slab")
    copies = []
    for index in range(count):
        pair = weights[2 * (index % 2) : 2 * (index % 2) + 2]
        which, place = places[index]
        slot_weights(homes_refs[which][place], slab, slots, grid_width, *pair)
        for half in range(2):
            high_ref, low_ref = tables[2 * half : 2 * half + 2]
            width = high_ref.shape[1]
            result = contract(pair, high_ref[...], low_ref[...])
            store_slots(staged[index], slice(half * width, (half + 1) * width), result, capacity, slots)
        copy = pltpu.make_async_copy(staged[index], outs[index], sems.at[index])
        copy.start()
        copies.append(copy)
    for copy in copies:
        copy.wait()


def place_kernel(capacity, slots, turn, packed_ref, *refs):
    pieces, (out_ref, placed, sems), landed = refs[:4], (refs[-7], *refs[-2:]), refs[-6:-2]
    slab, orb = lax.axis_index("slab"), lax.axis_index("orb")
    arrivals = [pltpu.make_async_copy(piece, buffer, sems.at[index]) for index, (piece, buffer) in enumerate(zip(pieces, landed))]
    for arrival in arrivals:
        arrival.start()
    electrons = out_ref.shape[1]
    width = out_ref.shape[2] // 4
    owner = to_column(packed_ref[5:6, :electrons])
    slot = to_column(packed_ref[6:7, :electrons])
    step = jnp.zeros_like(owner)
    for index in range(1, 4):
        step = jnp.where(owner == (slab ^ index).astype(F32), float(index), step)
    pick = (iota((electrons, 4 * slots), 1).astype(F32) == step * float(slots) + slot).astype(BF16)
    for arrival in arrivals:
        arrival.wait()
    departures = []
    for half in range(2):
        lanes = slice(half * width, (half + 1) * width)
        for k in range(5):
            rows = slice(k * capacity, k * capacity + slots)
            stack = jnp.concatenate([buffer[rows, lanes] for buffer in landed], axis=0)
            placed[half, k] = jnp.dot(pick, stack, preferred_element_type=F32).astype(BF16)
        start = pl.multiple_of((orb ^ (2 * turn + half)) * width, LANES)
        departure = pltpu.make_async_copy(placed.at[half], out_ref.at[:, :, pl.ds(start, width)], sems.at[4 + half])
        departure.start()
        departures.append(departure)
    for departure in departures:
        departure.wait()


def swap(array, step, count, axes):
    return lax.ppermute(array, axes, [(i, i ^ step) for i in range(count)])


def after(array, *others):
    return lax.optimization_barrier((array, *others))[0]


HBM = pl.BlockSpec(memory_space=pltpu.HBM)
VMEM = pl.BlockSpec(memory_space=pltpu.VMEM)


def small_body(fractions, cell_index, slab_owner, spline_table):
    electrons = slab_owner.shape[0]
    grid_width, planes, orb_local = spline_table.shape[1], spline_table.shape[3], spline_table.shape[4]
    capacity = slot_capacity(electrons, 4)
    slots = -(-capacity // 16) * 16
    rows, width = 4 * capacity + slots, 2 * orb_local
    taps = grid_width * grid_width * planes
    vmem = pltpu.CompilerParams(vmem_limit_bytes=40 * 1024 * 1024)
    blocks = functools.partial(jax.ShapeDtypeStruct, dtype=BF16)
    both_axes = ("slab", "orb")

    partner_table = swap(spline_table, 1, 4, "orb")
    packed = pl.pallas_call(
        pack_kernel, out_shape=jax.ShapeDtypeStruct((8, LANES), F32), name="pack"
    )(fractions, cell_index, slab_owner.reshape(1, electrons))
    def split(table):
        view = table.reshape(grid_width * grid_width, planes, orb_local // LANES, LANES)
        view = view.transpose(0, 2, 1, 3).reshape(taps * orb_local // LANES, LANES)
        return pl.pallas_call(
            functools.partial(split_kernel, planes),
            out_shape=[blocks((taps, orb_local))] * 2,
            in_specs=[HBM],
            scratch_shapes=[pltpu.VMEM(view.shape, F32), pltpu.SemaphoreType.DMA((8,))],
            compiler_params=vmem,
            name="split",
        )(view)

    along = [packed] + [swap(packed, step, 4, "slab") for step in (1, 2, 3)]
    tables = split(spline_table) + split(partner_table)
    straight = jnp.stack([after(packed, *tables)] + along[1:])
    crossed = swap(straight, 2, 4, "orb")

    first = after(along[2], along[1], along[3])

    def serve(name, homes, *places):
        count = len(places)
        return pl.pallas_call(
            functools.partial(serve_kernel, (capacity, slots, grid_width), places),
            out_shape=[blocks((rows, width))] * count,
            in_specs=[VMEM] * (4 + len(homes)),
            out_specs=[HBM] * count,
            scratch_shapes=[pltpu.VMEM((rows, width), BF16)] * count
            + [pltpu.VMEM((5 * slots, taps), BF16)] * 4
            + [pltpu.SemaphoreType.DMA((count,))],
            compiler_params=vmem,
            name=name,
        )(*tables, *homes)

    def send(step, block):
        return swap(block, step, 16, both_axes)

    across_out = serve("across", [first[None]], (0, 0))
    across_out += serve("across", [after(crossed, *across_out)], (0, 2))
    both = (after(straight, *across_out), crossed)
    corner_out = serve("corner", both, (0, 3), (1, 3))
    both = (after(straight, *corner_out), crossed)
    near_out = serve("near", both, (0, 0), (1, 0), (0, 1), (1, 1))
    far = [send(8 + 2 * index, block) for index, block in enumerate(across_out + corner_out)]
    near = [near_out[0]] + [send(2 * index, near_out[index]) for index in range(1, 4)]
    out = ()
    for turn in range(2):
        pieces = near[turn::2] + far[turn::2]
        out = pl.pallas_call(
            functools.partial(place_kernel, capacity, slots, turn),
            out_shape=[blocks((5, electrons, 4 * orb_local))],
            in_specs=[VMEM] + [HBM] * (4 + len(out)),
            out_specs=[HBM],
            input_output_aliases={5: 0} if out else {},
            scratch_shapes=[pltpu.VMEM((rows, width), BF16)] * 4
            + [pltpu.VMEM((2, 5, electrons, orb_local), BF16), pltpu.SemaphoreType.DMA((6,))],
            compiler_params=vmem,
            name="place",
        )(packed, *pieces, *out)
    return out[0]


def solution(mesh):
    in_specs = (
        P(None, ("groups", "slab", "orb")),
        P(None, ("groups", "slab", "orb")),
        P(("groups", "slab", "orb"), None),
        P("slab", None, None, None, "orb"),
    )
    out_specs = P(None, ("groups", "slab", "orb"), None)
    small = (mesh.shape["groups"], mesh.shape["slab"], mesh.shape["orb"]) == (2, 4, 4)
    body = small_body if small else general_body
    return jax.shard_map(body, mesh=mesh, in_specs=in_specs, out_specs=out_specs, check_vma=False)
```

```python
import functools

import jax
import jax.numpy as jnp
from jax import lax
from jax.experimental import pallas as pl
from jax.experimental.pallas import tpu as pltpu
from jax.sharding import PartitionSpec as P

LANES = 128
F32 = jnp.float32
BF16 = jnp.bfloat16


def spline_taps(position):
    remain = 1.0 - position
    square = position * position
    frac_cube = square * position
    values = (
        remain * remain * remain / 6.0,
        (3.0 * frac_cube - 6.0 * square + 4.0) / 6.0,
        (-3.0 * frac_cube + 3.0 * square + 3.0 * position + 1.0) / 6.0,
        frac_cube / 6.0,
    )
    slopes = (
        -0.5 * remain * remain,
        0.5 * (3.0 * square - 4.0 * position),
        0.5 * (-3.0 * square + 2.0 * position + 1.0),
        0.5 * square,
    )
    curves = (remain, 3.0 * position - 2.0, 1.0 - 3.0 * position, position)
    return values, slopes, curves


def spline_bases(position):
    return tuple(jnp.stack(taps, axis=-1) for taps in spline_taps(position))


def spread_taps(first_cell, taps, grid_width):
    offsets = jnp.arange(4, dtype=jnp.int32)
    cells = jnp.arange(grid_width, dtype=jnp.int32)
    wrapped = (first_cell[:, None] + offsets[None, :]) % grid_width
    hits = (wrapped[:, :, None] == cells[None, None, :]).astype(jnp.float32)
    return jnp.sum(hits * taps[:, :, None], axis=1)


def evaluate(incoming, table_flat, grid_width):
    basis_x, slope_x, curve_x = spline_bases(incoming[0])
    basis_y, slope_y, curve_y = spline_bases(incoming[1])
    basis_z, slope_z, curve_z = spline_bases(incoming[2])
    row_y = incoming[3].astype(jnp.int32)
    row_z = incoming[4].astype(jnp.int32)
    value_y = spread_taps(row_y, basis_y, grid_width)[:, :, None, None]
    deriv_y = spread_taps(row_y, slope_y, grid_width)[:, :, None, None]
    second_y = spread_taps(row_y, curve_y, grid_width)[:, :, None, None]
    value_z = spread_taps(row_z, basis_z, grid_width)[:, None, :, None]
    deriv_z = spread_taps(row_z, slope_z, grid_width)[:, None, :, None]
    second_z = spread_taps(row_z, curve_z, grid_width)[:, None, :, None]
    value_x = basis_x[:, None, None, :]
    deriv_x = slope_x[:, None, None, :]
    second_x = curve_x[:, None, None, :]
    dense = jnp.stack(
        [
            value_x * value_y * value_z,
            deriv_x * value_y * value_z,
            value_x * deriv_y * value_z,
            value_x * value_y * deriv_z,
            second_x * value_y * value_z
            + value_x * second_y * value_z
            + value_x * value_y * second_z,
        ]
    )
    slot_count = incoming.shape[1]
    dense = dense.reshape(5 * slot_count, table_flat.shape[0])
    result = jnp.dot(
        dense, table_flat, precision=lax.Precision.HIGHEST, preferred_element_type=jnp.float32
    )
    return result.reshape(5, slot_count, table_flat.shape[1]).astype(jnp.bfloat16)


def slot_capacity(electrons, slab_count):
    return max(2, (5 * electrons + 4 * slab_count - 1) // (4 * slab_count))


def general_body(fractions, cell_index, slab_owner, spline_table):
    slab_count = lax.axis_size("slab")
    orb_count = lax.axis_size("orb")
    electrons = slab_owner.shape[0]
    capacity = slot_capacity(electrons, slab_count)
    grid_width = spline_table.shape[1]
    orb_local = spline_table.shape[4]
    owners = slab_owner[:, 0]
    columns = jnp.arange(slab_count, dtype=jnp.int32)
    member = (owners[:, None] == columns[None, :]).astype(jnp.int32)
    earlier = jnp.cumsum(member, axis=0) - member
    slot_place = owners * capacity + jnp.sum(earlier * member, axis=1)
    packed = jnp.concatenate([fractions, cell_index.astype(jnp.float32)], axis=0)
    outgoing = jnp.zeros((5, slab_count * capacity), jnp.float32).at[:, slot_place].set(packed)
    outgoing = outgoing.reshape(5, 1, slab_count, capacity)
    spread = lax.all_gather(outgoing, "orb", axis=1, tiled=True)
    arrived = lax.all_to_all(spread, "slab", split_axis=2, concat_axis=2, tiled=True)
    table_flat = spline_table.reshape(grid_width * grid_width * 4, orb_local)
    per_source = jnp.moveaxis(arrived.reshape(5, orb_count, slab_count * capacity), 1, 0)
    blocks = lax.map(lambda incoming: evaluate(incoming, table_flat, grid_width), per_source)
    results = jnp.moveaxis(blocks, 0, 1).reshape(5, orb_count, slab_count, capacity, orb_local)
    returned = lax.all_to_all(results, "slab", split_axis=2, concat_axis=2, tiled=True)
    at_home = lax.all_to_all(returned, "orb", split_axis=1, concat_axis=4, tiled=True)
    flat_home = at_home.reshape(5, slab_count * capacity, at_home.shape[4])
    return jnp.take(flat_home, slot_place, axis=1)


def iota(shape, dim):
    return lax.broadcasted_iota(jnp.int32, shape, dim)


def to_column(row):
    count = row.shape[1]
    spread = jnp.broadcast_to(row, (count, count))
    return jnp.sum(jnp.where(iota((count, count), 0) == iota((count, count), 1), spread, 0.0), axis=1, keepdims=True)


def pack_kernel(fractions_ref, cells_ref, owner_ref, packed_ref):
    electrons = fractions_ref.shape[1]
    owner = owner_ref[...].astype(F32)
    same = to_column(owner) == owner
    before = iota((electrons, electrons), 0) < iota((electrons, electrons), 1)
    slot = jnp.sum(jnp.where(same & before, 1.0, 0.0), axis=0, keepdims=True)
    packed_ref[...] = jnp.full(packed_ref.shape, -1.0, F32)
    packed_ref[0:3, :electrons] = fractions_ref[...]
    packed_ref[3:5, :electrons] = cells_ref[...].astype(F32)
    packed_ref[5:6, :electrons] = owner
    packed_ref[6:7, :electrons] = slot


def split_kernel(planes, table_ref, high_ref, low_ref, landed, sems):
    blocks = high_ref.shape[1] // LANES
    pieces = sems.shape[0]
    piece = table_ref.shape[0] // pieces
    count = piece // (blocks * planes)
    copies = []
    for index in range(pieces):
        span = slice(index * piece, (index + 1) * piece)
        copies.append(pltpu.make_async_copy(table_ref.at[span, :], landed.at[span, :], sems.at[index]))
        copies[-1].start()
    for index in range(pieces):
        copies[index].wait()
        for block in range(blocks):
            lanes = slice(block * LANES, (block + 1) * LANES)
            for plane in range(planes):
                first = index * piece + block * planes + plane
                table = landed[pl.ds(first, count, stride=blocks * planes), :]
                high = table.astype(BF16)
                start = (plane * pieces + index) * count
                high_ref[start : start + count, lanes] = high
                low_ref[start : start + count, lanes] = (table - high.astype(F32)).astype(BF16)


def slot_weights(home, slab, slots, grid_width, high_ref, low_ref):
    owner, slot = home[5:6, :], home[6:7, :]
    wanted = jnp.where(owner == slab.astype(F32), slot, -1.0)
    chosen = iota((slots, LANES), 0).astype(F32) == wanted
    lane = iota((slots, LANES), 1)

    def field(index):
        picked = jnp.sum(jnp.where(chosen, home[index : index + 1, :], 0.0), axis=1, keepdims=True)
        return jnp.broadcast_to(picked, (slots, LANES))

    (x_value, x_slope, x_curve), taps_y, taps_z = (spline_taps(field(dim)) for dim in range(3))
    first_y, first_z = field(3).astype(jnp.int32), field(4).astype(jnp.int32)

    def pick(offset, kinds):
        hits = [offset == tap for tap in range(4)]
        picked = []
        for taps in kinds:
            out = jnp.where(hits[3], taps[3], 0.0)
            for tap in (2, 1, 0):
                out = jnp.where(hits[tap], taps[tap], out)
            picked.append(out)
        return picked

    z_value, z_slope, z_curve = pick(((lane & (grid_width - 1)) - first_z) & (grid_width - 1), taps_z)
    per_chunk = LANES // grid_width
    for chunk in range(grid_width // per_chunk):
        offset_y = (chunk * per_chunk + lane // grid_width - first_y) & (grid_width - 1)
        y_value, y_slope, y_curve = pick(offset_y, taps_y)
        plain = y_value * z_value
        with_y = y_slope * z_value
        with_z = y_value * z_slope
        with_both = y_curve * z_value + y_value * z_curve
        for plane in range(4):
            weights = (
                x_value[plane] * plain,
                x_slope[plane] * plain,
                x_value[plane] * with_y,
                x_value[plane] * with_z,
                x_curve[plane] * plain + x_value[plane] * with_both,
            )
            start = plane * grid_width * grid_width + chunk * LANES
            for k, weight in enumerate(weights):
                high = weight.astype(BF16)
                high_ref[k * slots : (k + 1) * slots, start : start + LANES] = high
                low_ref[k * slots : (k + 1) * slots, start : start + LANES] = (weight - high.astype(F32)).astype(BF16)


def contract(weights, table_high, table_low):
    dot = functools.partial(jnp.dot, preferred_element_type=F32)
    high, low = weights[0][...], weights[1][...]
    return dot(high, table_high) + (dot(low, table_high) + dot(high, table_low))


def store_slots(out_ref, lanes, result, capacity, slots):
    for k in range(5):
        out_ref[k * capacity : k * capacity + slots, lanes] = result[k * slots : (k + 1) * slots].astype(BF16)


def serve_kernel(sizes, places, *refs):
    capacity, slots, grid_width = sizes
    count = len(places)
    weights, sems = refs[-5:-1], refs[-1]
    tables, homes_refs, outs, staged = refs[:4], refs[4 : -5 - 2 * count], refs[-5 - 2 * count : -5 - count], refs[-5 - count : -5]
    slab = lax.axis_index("slab")
    copies = []
    for index in range(count):
        pair = weights[2 * (index % 2) : 2 * (index % 2) + 2]
        which, place = places[index]
        slot_weights(homes_refs[which][place], slab, slots, grid_width, *pair)
        for half in range(2):
            high_ref, low_ref = tables[2 * half : 2 * half + 2]
            width = high_ref.shape[1]
            result = contract(pair, high_ref[...], low_ref[...])
            store_slots(staged[index], slice(half * width, (half + 1) * width), result, capacity, slots)
        copy = pltpu.make_async_copy(staged[index], outs[index], sems.at[index])
        copy.start()
        copies.append(copy)
    for copy in copies:
        copy.wait()


def place_kernel(capacity, slots, turn, packed_ref, *refs):
    pieces, (out_ref, placed, sems), landed = refs[:4], (refs[-7], *refs[-2:]), refs[-6:-2]
    slab, orb = lax.axis_index("slab"), lax.axis_index("orb")
    width = out_ref.shape[2] // 4
    arrivals = []
    for half in range(2):
        lanes = slice(half * width, (half + 1) * width)
        for index in range(4):
            arrival = pltpu.make_async_copy(pieces[index].at[:, lanes], landed[index].at[:, lanes], sems.at[4 * half + index])
            arrival.start()
            arrivals.append(arrival)
    electrons = out_ref.shape[1]
    owner = to_column(packed_ref[5:6, :electrons])
    slot = to_column(packed_ref[6:7, :electrons])
    step = jnp.zeros_like(owner)
    for index in range(1, 4):
        step = jnp.where(owner == (slab ^ index).astype(F32), float(index), step)
    pick = (iota((electrons, 4 * slots), 1).astype(F32) == step * float(slots) + slot).astype(BF16)
    departures = []
    for half in range(2):
        lanes = slice(half * width, (half + 1) * width)
        for arrival in arrivals[4 * half : 4 * half + 4]:
            arrival.wait()
        for k in range(5):
            rows = slice(k * capacity, k * capacity + slots)
            stack = jnp.concatenate([buffer[rows, lanes] for buffer in landed], axis=0)
            placed[half, k] = jnp.dot(pick, stack, preferred_element_type=F32).astype(BF16)
        start = pl.multiple_of((orb ^ (2 * turn + half)) * width, LANES)
        departure = pltpu.make_async_copy(placed.at[half], out_ref.at[:, :, pl.ds(start, width)], sems.at[8 + half])
        departure.start()
        departures.append(departure)
    for departure in departures:
        departure.wait()


def swap(array, step, count, axes):
    return lax.ppermute(array, axes, [(i, i ^ step) for i in range(count)])


def after(array, *others):
    return lax.optimization_barrier((array, *others))[0]


HBM = pl.BlockSpec(memory_space=pltpu.HBM)
VMEM = pl.BlockSpec(memory_space=pltpu.VMEM)


def small_body(fractions, cell_index, slab_owner, spline_table):
    electrons = slab_owner.shape[0]
    grid_width, planes, orb_local = spline_table.shape[1], spline_table.shape[3], spline_table.shape[4]
    capacity = slot_capacity(electrons, 4)
    slots = -(-capacity // 16) * 16
    rows, width = 4 * capacity + slots, 2 * orb_local
    taps = grid_width * grid_width * planes
    vmem = pltpu.CompilerParams(vmem_limit_bytes=40 * 1024 * 1024)
    blocks = functools.partial(jax.ShapeDtypeStruct, dtype=BF16)
    both_axes = ("slab", "orb")

    partner_table = swap(spline_table, 1, 4, "orb")
    packed = pl.pallas_call(
        pack_kernel, out_shape=jax.ShapeDtypeStruct((8, LANES), F32), name="pack"
    )(fractions, cell_index, slab_owner.reshape(1, electrons))
    def split(table):
        view = table.reshape(grid_width * grid_width, planes, orb_local // LANES, LANES)
        view = view.transpose(0, 2, 1, 3).reshape(taps * orb_local // LANES, LANES)
        return pl.pallas_call(
            functools.partial(split_kernel, planes),
            out_shape=[blocks((taps, orb_local))] * 2,
            in_specs=[HBM],
            scratch_shapes=[pltpu.VMEM(view.shape, F32), pltpu.SemaphoreType.DMA((8,))],
            compiler_params=vmem,
            name="split",
        )(view)

    def split(table):
        view = table.reshape(grid_width * grid_width, planes, orb_local // LANES, LANES)
        view = view.transpose(0, 2, 1, 3).reshape(taps * orb_local // LANES, LANES)
        return pl.pallas_call(
            functools.partial(split_kernel, planes),
            out_shape=[blocks((taps, orb_local))] * 2,
            in_specs=[HBM],
            scratch_shapes=[pltpu.VMEM(view.shape, F32), pltpu.SemaphoreType.DMA((8,))],
            compiler_params=vmem,
            name="split",
        )(view)

    along = [packed] + [swap(packed, step, 4, "slab") for step in (1, 2, 3)]
    tables = split(spline_table) + split(partner_table)
    pair = jnp.stack([after(packed, *tables), swap(packed, 2, 4, "slab")])
    side = swap(pair, 1, 4, "slab")

    def serve(name, homes, *places):
        count = len(places)
        return pl.pallas_call(
            functools.partial(serve_kernel, (capacity, slots, grid_width), places),
            out_shape=[blocks((rows, width))] * count,
            in_specs=[VMEM] * (4 + len(homes)),
            out_specs=[HBM] * count,
            scratch_shapes=[pltpu.VMEM((rows, width), BF16)] * count
            + [pltpu.VMEM((5 * slots, taps), BF16)] * 4
            + [pltpu.SemaphoreType.DMA((count,))],
            compiler_params=vmem,
            name=name,
        )(*tables, *homes)

    def send(step, block):
        return swap(block, step, 16, both_axes)

    across_out = serve("across", [pair], (0, 1))
    straight = jnp.stack([after(pair, *across_out), side])
    crossed = swap(straight, 2, 4, "orb")
    across_out += serve("across", [after(crossed, *across_out)], (0, (0, 1)))
    both = (after(straight, *across_out), crossed)
    corner_out = serve("corner", both, (0, (1, 1)), (1, (1, 1)))
    both = (after(straight, *corner_out), crossed)
    near_out = serve("near", both, (0, (0, 0)), (1, (0, 0)), (0, (1, 0)), (1, (1, 0)))
    far = [send(8 + 2 * index, block) for index, block in enumerate(across_out + corner_out)]
    near = [near_out[0]] + [send(2 * index, near_out[index]) for index in range(1, 4)]
    out = ()
    for turn in range(2):
        pieces = near[turn::2] + far[turn::2]
        out = pl.pallas_call(
            functools.partial(place_kernel, capacity, slots, turn),
            out_shape=[blocks((5, electrons, 4 * orb_local))],
            in_specs=[VMEM] + [HBM] * (4 + len(out)),
            out_specs=[HBM],
            input_output_aliases={5: 0} if out else {},
            scratch_shapes=[pltpu.VMEM((rows, width), BF16)] * 4
            + [pltpu.VMEM((2, 5, electrons, orb_local), BF16), pltpu.SemaphoreType.DMA((10,))],
            compiler_params=vmem,
            name="place",
        )(packed, *pieces, *out)
    return out[0]


def solution(mesh):
    in_specs = (
        P(None, ("groups", "slab", "orb")),
        P(None, ("groups", "slab", "orb")),
        P(("groups", "slab", "orb"), None),
        P("slab", None, None, None, "orb"),
    )
    out_specs = P(None, ("groups", "slab", "orb"), None)
    small = (mesh.shape["groups"], mesh.shape["slab"], mesh.shape["orb"]) == (2, 4, 4)
    body = small_body if small else general_body
    return jax.shard_map(body, mesh=mesh, in_specs=in_specs, out_specs=out_specs, check_vma=False)
```

```python
import functools

import jax
import jax.numpy as jnp
from jax import lax
from jax.experimental import pallas as pl
from jax.experimental.pallas import tpu as pltpu
from jax.sharding import PartitionSpec as P

LANES = 128
F32 = jnp.float32
BF16 = jnp.bfloat16


def spline_taps(position):
    remain = 1.0 - position
    square = position * position
    frac_cube = square * position
    values = (
        remain * remain * remain / 6.0,
        (3.0 * frac_cube - 6.0 * square + 4.0) / 6.0,
        (-3.0 * frac_cube + 3.0 * square + 3.0 * position + 1.0) / 6.0,
        frac_cube / 6.0,
    )
    slopes = (
        -0.5 * remain * remain,
        0.5 * (3.0 * square - 4.0 * position),
        0.5 * (-3.0 * square + 2.0 * position + 1.0),
        0.5 * square,
    )
    curves = (remain, 3.0 * position - 2.0, 1.0 - 3.0 * position, position)
    return values, slopes, curves


def spline_bases(position):
    return tuple(jnp.stack(taps, axis=-1) for taps in spline_taps(position))


def spread_taps(first_cell, taps, grid_width):
    offsets = jnp.arange(4, dtype=jnp.int32)
    cells = jnp.arange(grid_width, dtype=jnp.int32)
    wrapped = (first_cell[:, None] + offsets[None, :]) % grid_width
    hits = (wrapped[:, :, None] == cells[None, None, :]).astype(jnp.float32)
    return jnp.sum(hits * taps[:, :, None], axis=1)


def evaluate(incoming, table_flat, grid_width):
    basis_x, slope_x, curve_x = spline_bases(incoming[0])
    basis_y, slope_y, curve_y = spline_bases(incoming[1])
    basis_z, slope_z, curve_z = spline_bases(incoming[2])
    row_y = incoming[3].astype(jnp.int32)
    row_z = incoming[4].astype(jnp.int32)
    value_y = spread_taps(row_y, basis_y, grid_width)[:, :, None, None]
    deriv_y = spread_taps(row_y, slope_y, grid_width)[:, :, None, None]
    second_y = spread_taps(row_y, curve_y, grid_width)[:, :, None, None]
    value_z = spread_taps(row_z, basis_z, grid_width)[:, None, :, None]
    deriv_z = spread_taps(row_z, slope_z, grid_width)[:, None, :, None]
    second_z = spread_taps(row_z, curve_z, grid_width)[:, None, :, None]
    value_x = basis_x[:, None, None, :]
    deriv_x = slope_x[:, None, None, :]
    second_x = curve_x[:, None, None, :]
    dense = jnp.stack(
        [
            value_x * value_y * value_z,
            deriv_x * value_y * value_z,
            value_x * deriv_y * value_z,
            value_x * value_y * deriv_z,
            second_x * value_y * value_z
            + value_x * second_y * value_z
            + value_x * value_y * second_z,
        ]
    )
    slot_count = incoming.shape[1]
    dense = dense.reshape(5 * slot_count, table_flat.shape[0])
    result = jnp.dot(
        dense, table_flat, precision=lax.Precision.HIGHEST, preferred_element_type=jnp.float32
    )
    return result.reshape(5, slot_count, table_flat.shape[1]).astype(jnp.bfloat16)


def slot_capacity(electrons, slab_count):
    return max(2, (5 * electrons + 4 * slab_count - 1) // (4 * slab_count))


def general_body(fractions, cell_index, slab_owner, spline_table):
    slab_count = lax.axis_size("slab")
    orb_count = lax.axis_size("orb")
    electrons = slab_owner.shape[0]
    capacity = slot_capacity(electrons, slab_count)
    grid_width = spline_table.shape[1]
    orb_local = spline_table.shape[4]
    owners = slab_owner[:, 0]
    columns = jnp.arange(slab_count, dtype=jnp.int32)
    member = (owners[:, None] == columns[None, :]).astype(jnp.int32)
    earlier = jnp.cumsum(member, axis=0) - member
    slot_place = owners * capacity + jnp.sum(earlier * member, axis=1)
    packed = jnp.concatenate([fractions, cell_index.astype(jnp.float32)], axis=0)
    outgoing = jnp.zeros((5, slab_count * capacity), jnp.float32).at[:, slot_place].set(packed)
    outgoing = outgoing.reshape(5, 1, slab_count, capacity)
    spread = lax.all_gather(outgoing, "orb", axis=1, tiled=True)
    arrived = lax.all_to_all(spread, "slab", split_axis=2, concat_axis=2, tiled=True)
    table_flat = spline_table.reshape(grid_width * grid_width * 4, orb_local)
    per_source = jnp.moveaxis(arrived.reshape(5, orb_count, slab_count * capacity), 1, 0)
    blocks = lax.map(lambda incoming: evaluate(incoming, table_flat, grid_width), per_source)
    results = jnp.moveaxis(blocks, 0, 1).reshape(5, orb_count, slab_count, capacity, orb_local)
    returned = lax.all_to_all(results, "slab", split_axis=2, concat_axis=2, tiled=True)
    at_home = lax.all_to_all(returned, "orb", split_axis=1, concat_axis=4, tiled=True)
    flat_home = at_home.reshape(5, slab_count * capacity, at_home.shape[4])
    return jnp.take(flat_home, slot_place, axis=1)


def iota(shape, dim):
    return lax.broadcasted_iota(jnp.int32, shape, dim)


def to_column(row):
    count = row.shape[1]
    spread = jnp.broadcast_to(row, (count, count))
    return jnp.sum(jnp.where(iota((count, count), 0) == iota((count, count), 1), spread, 0.0), axis=1, keepdims=True)


def pack_kernel(fractions_ref, cells_ref, owner_ref, packed_ref):
    electrons = fractions_ref.shape[1]
    owner = owner_ref[...].astype(F32)
    same = to_column(owner) == owner
    before = iota((electrons, electrons), 0) < iota((electrons, electrons), 1)
    slot = jnp.sum(jnp.where(same & before, 1.0, 0.0), axis=0, keepdims=True)
    packed_ref[...] = jnp.full(packed_ref.shape, -1.0, F32)
    packed_ref[0:3, :electrons] = fractions_ref[...]
    packed_ref[3:5, :electrons] = cells_ref[...].astype(F32)
    packed_ref[5:6, :electrons] = owner
    packed_ref[6:7, :electrons] = slot


def split_kernel(planes, table_ref, high_ref, low_ref):
    blocks = high_ref.shape[1] // LANES
    count = table_ref.shape[0] // (blocks * planes)
    for block in range(blocks):
        for plane in range(planes):
            table = table_ref[pl.ds(block * planes + plane, count, stride=blocks * planes), :]
            high = table.astype(BF16)
            rows, lanes = slice(plane * count, (plane + 1) * count), slice(block * LANES, (block + 1) * LANES)
            high_ref[rows, lanes] = high
            low_ref[rows, lanes] = (table - high.astype(F32)).astype(BF16)


def slot_weights(home, slab, slots, grid_width, high_ref, low_ref):
    owner, slot = home[5:6, :], home[6:7, :]
    wanted = jnp.where(owner == slab.astype(F32), slot, -1.0)
    chosen = iota((slots, LANES), 0).astype(F32) == wanted
    lane = iota((slots, LANES), 1)

    def field(index):
        picked = jnp.sum(jnp.where(chosen, home[index : index + 1, :], 0.0), axis=1, keepdims=True)
        return jnp.broadcast_to(picked, (slots, LANES))

    (x_value, x_slope, x_curve), taps_y, taps_z = (spline_taps(field(dim)) for dim in range(3))
    first_y, first_z = field(3).astype(jnp.int32), field(4).astype(jnp.int32)

    def pick(offset, kinds):
        hits = [offset == tap for tap in range(4)]
        picked = []
        for taps in kinds:
            out = jnp.where(hits[3], taps[3], 0.0)
            for tap in (2, 1, 0):
                out = jnp.where(hits[tap], taps[tap], out)
            picked.append(out)
        return picked

    z_value, z_slope, z_curve = pick(((lane & (grid_width - 1)) - first_z) & (grid_width - 1), taps_z)
    per_chunk = LANES // grid_width
    for chunk in range(grid_width // per_chunk):
        offset_y = (chunk * per_chunk + lane // grid_width - first_y) & (grid_width - 1)
        y_value, y_slope, y_curve = pick(offset_y, taps_y)
        plain = y_value * z_value
        with_y = y_slope * z_value
        with_z = y_value * z_slope
        with_both = y_curve * z_value + y_value * z_curve
        for plane in range(4):
            weights = (
                x_value[plane] * plain,
                x_slope[plane] * plain,
                x_value[plane] * with_y,
                x_value[plane] * with_z,
                x_curve[plane] * plain + x_value[plane] * with_both,
            )
            start = plane * grid_width * grid_width + chunk * LANES
            for k, weight in enumerate(weights):
                high = weight.astype(BF16)
                high_ref[k * slots : (k + 1) * slots, start : start + LANES] = high
                low_ref[k * slots : (k + 1) * slots, start : start + LANES] = (weight - high.astype(F32)).astype(BF16)


def contract(weights, table_high, table_low):
    dot = functools.partial(jnp.dot, preferred_element_type=F32)
    high, low = weights[0][...], weights[1][...]
    return dot(high, table_high) + (dot(low, table_high) + dot(high, table_low))


def store_slots(out_ref, lanes, result, capacity, slots):
    for k in range(5):
        out_ref[k * capacity : k * capacity + slots, lanes] = result[k * slots : (k + 1) * slots].astype(BF16)


def serve_kernel(sizes, places, *refs):
    capacity, slots, grid_width = sizes
    count = len(places)
    tables, homes_refs, outs, weights = refs[:4], refs[4 : -4 - count], refs[-4 - count : -4], refs[-4:]
    slab = lax.axis_index("slab")
    for index in range(count):
        pair = weights[2 * (index % 2) : 2 * (index % 2) + 2]
        which, place = places[index]
        slot_weights(homes_refs[which][place], slab, slots, grid_width, *pair)
        for half in range(2):
            high_ref, low_ref = tables[2 * half : 2 * half + 2]
            width = high_ref.shape[1]
            result = contract(pair, high_ref[...], low_ref[...])
            store_slots(outs[index], slice(half * width, (half + 1) * width), result, capacity, slots)


def place_kernel(capacity, slots, turn, packed_ref, *refs):
    pieces, (out_ref, placed, sems) = refs[:4], refs[-3:]
    slab, orb = lax.axis_index("slab"), lax.axis_index("orb")
    width = out_ref.shape[2] // 4
    electrons = out_ref.shape[1]
    owner = to_column(packed_ref[5:6, :electrons])
    slot = to_column(packed_ref[6:7, :electrons])
    step = jnp.zeros_like(owner)
    for index in range(1, 4):
        step = jnp.where(owner == (slab ^ index).astype(F32), float(index), step)
    pick = (iota((electrons, 4 * slots), 1).astype(F32) == step * float(slots) + slot).astype(BF16)
    departures = []
    for half in range(2):
        lanes = slice(half * width, (half + 1) * width)
        for k in range(5):
            rows = slice(k * capacity, k * capacity + slots)
            stack = jnp.concatenate([buffer[rows, lanes] for buffer in pieces], axis=0)
            placed[half, k] = jnp.dot(pick, stack, preferred_element_type=F32).astype(BF16)
        start = pl.multiple_of((orb ^ (2 * turn + half)) * width, LANES)
        departure = pltpu.make_async_copy(placed.at[half], out_ref.at[:, :, pl.ds(start, width)], sems.at[half])
        departure.start()
        departures.append(departure)
    for departure in departures:
        departure.wait()


def swap(array, step, count, axes):
    return lax.ppermute(array, axes, [(i, i ^ step) for i in range(count)])


def after(array, *others):
    return lax.optimization_barrier((array, *others))[0]


HBM = pl.BlockSpec(memory_space=pltpu.HBM)
VMEM = pl.BlockSpec(memory_space=pltpu.VMEM)


def small_body(fractions, cell_index, slab_owner, spline_table):
    electrons = slab_owner.shape[0]
    grid_width, planes, orb_local = spline_table.shape[1], spline_table.shape[3], spline_table.shape[4]
    capacity = slot_capacity(electrons, 4)
    slots = -(-capacity // 16) * 16
    rows, width = 4 * capacity + slots, 2 * orb_local
    taps = grid_width * grid_width * planes
    vmem = pltpu.CompilerParams(vmem_limit_bytes=40 * 1024 * 1024)
    blocks = functools.partial(jax.ShapeDtypeStruct, dtype=BF16)
    both_axes = ("slab", "orb")

    partner_table = swap(spline_table, 1, 4, "orb")
    packed = pl.pallas_call(
        pack_kernel, out_shape=jax.ShapeDtypeStruct((8, LANES), F32), name="pack"
    )(fractions, cell_index, slab_owner.reshape(1, electrons))
    def split(table):
        view = table.reshape(grid_width * grid_width, planes, orb_local // LANES, LANES)
        view = view.transpose(0, 2, 1, 3).reshape(taps * orb_local // LANES, LANES)
        return pl.pallas_call(
            functools.partial(split_kernel, planes),
            out_shape=[blocks((taps, orb_local))] * 2,
            compiler_params=vmem,
            name="split",
        )(view)

    def split(table):
        view = table.reshape(grid_width * grid_width, planes, orb_local // LANES, LANES)
        view = view.transpose(0, 2, 1, 3).reshape(taps * orb_local // LANES, LANES)
        return pl.pallas_call(
            functools.partial(split_kernel, planes),
            out_shape=[blocks((taps, orb_local))] * 2,
            compiler_params=vmem,
            name="split",
        )(view)

    along = [packed] + [swap(packed, step, 4, "slab") for step in (1, 2, 3)]
    tables = split(spline_table) + split(partner_table)
    pair = jnp.stack([after(packed, *tables), swap(packed, 2, 4, "slab")])
    side = swap(pair, 1, 4, "slab")

    def serve(name, homes, *places):
        count = len(places)
        return pl.pallas_call(
            functools.partial(serve_kernel, (capacity, slots, grid_width), places),
            out_shape=[blocks((rows, width))] * count,
            in_specs=[VMEM] * (4 + len(homes)),
            out_specs=[VMEM] * count,
            scratch_shapes=[pltpu.VMEM((5 * slots, taps), BF16)] * 4,
            compiler_params=vmem,
            name=name,
        )(*tables, *homes)

    def send(step, block):
        return swap(block, step, 16, both_axes)

    across_out = serve("across", [pair], (0, 1))
    straight = jnp.stack([after(pair, *across_out), side])
    crossed = swap(straight, 2, 4, "orb")
    across_out += serve("across", [after(crossed, *across_out)], (0, (0, 1)))
    both = (after(straight, *across_out), crossed)
    corner_out = serve("corner", both, (0, (1, 1)), (1, (1, 1)))
    both = (after(straight, *corner_out), crossed)
    near_out = serve("near", both, (0, (0, 0)), (1, (0, 0)), (0, (1, 0)), (1, (1, 0)))
    far = [send(8 + 2 * index, block) for index, block in enumerate(across_out + corner_out)]
    near = [near_out[0]] + [send(2 * index, near_out[index]) for index in range(1, 4)]
    out = ()
    for turn in range(2):
        pieces = near[turn::2] + far[turn::2]
        out = pl.pallas_call(
            functools.partial(place_kernel, capacity, slots, turn),
            out_shape=[blocks((5, electrons, 4 * orb_local))],
            in_specs=[VMEM] * 5 + [HBM] * len(out),
            out_specs=[HBM],
            input_output_aliases={5: 0} if out else {},
            scratch_shapes=[pltpu.VMEM((2, 5, electrons, orb_local), BF16), pltpu.SemaphoreType.DMA((2,))],
            compiler_params=vmem,
            name="place",
        )(packed, *pieces, *out)
    return out[0]


def solution(mesh):
    in_specs = (
        P(None, ("groups", "slab", "orb")),
        P(None, ("groups", "slab", "orb")),
        P(("groups", "slab", "orb"), None),
        P("slab", None, None, None, "orb"),
    )
    out_specs = P(None, ("groups", "slab", "orb"), None)
    small = (mesh.shape["groups"], mesh.shape["slab"], mesh.shape["orb"]) == (2, 4, 4)
    body = small_body if small else general_body
    return jax.shard_map(body, mesh=mesh, in_specs=in_specs, out_specs=out_specs, check_vma=False)
```

```python
import functools

import jax
import jax.numpy as jnp
from jax import lax
from jax.experimental import pallas as pl
from jax.experimental.pallas import tpu as pltpu
from jax.sharding import PartitionSpec as P

LANES = 128
BAND = 256
F32 = jnp.float32
BF16 = jnp.bfloat16


def spline_taps(position):
    remain = 1.0 - position
    square = position * position
    frac_cube = square * position
    values = (
        remain * remain * remain / 6.0,
        (3.0 * frac_cube - 6.0 * square + 4.0) / 6.0,
        (-3.0 * frac_cube + 3.0 * square + 3.0 * position + 1.0) / 6.0,
        frac_cube / 6.0,
    )
    slopes = (
        -0.5 * remain * remain,
        0.5 * (3.0 * square - 4.0 * position),
        0.5 * (-3.0 * square + 2.0 * position + 1.0),
        0.5 * square,
    )
    curves = (remain, 3.0 * position - 2.0, 1.0 - 3.0 * position, position)
    return values, slopes, curves


def spline_bases(position):
    return tuple(jnp.stack(taps, axis=-1) for taps in spline_taps(position))


def spread_taps(first_cell, taps, grid_width):
    offsets = jnp.arange(4, dtype=jnp.int32)
    cells = jnp.arange(grid_width, dtype=jnp.int32)
    wrapped = (first_cell[:, None] + offsets[None, :]) % grid_width
    hits = (wrapped[:, :, None] == cells[None, None, :]).astype(jnp.float32)
    return jnp.sum(hits * taps[:, :, None], axis=1)


def evaluate(incoming, table_flat, grid_width):
    basis_x, slope_x, curve_x = spline_bases(incoming[0])
    basis_y, slope_y, curve_y = spline_bases(incoming[1])
    basis_z, slope_z, curve_z = spline_bases(incoming[2])
    row_y = incoming[3].astype(jnp.int32)
    row_z = incoming[4].astype(jnp.int32)
    value_y = spread_taps(row_y, basis_y, grid_width)[:, :, None, None]
    deriv_y = spread_taps(row_y, slope_y, grid_width)[:, :, None, None]
    second_y = spread_taps(row_y, curve_y, grid_width)[:, :, None, None]
    value_z = spread_taps(row_z, basis_z, grid_width)[:, None, :, None]
    deriv_z = spread_taps(row_z, slope_z, grid_width)[:, None, :, None]
    second_z = spread_taps(row_z, curve_z, grid_width)[:, None, :, None]
    value_x = basis_x[:, None, None, :]
    deriv_x = slope_x[:, None, None, :]
    second_x = curve_x[:, None, None, :]
    dense = jnp.stack(
        [
            value_x * value_y * value_z,
            deriv_x * value_y * value_z,
            value_x * deriv_y * value_z,
            value_x * value_y * deriv_z,
            second_x * value_y * value_z
            + value_x * second_y * value_z
            + value_x * value_y * second_z,
        ]
    )
    slot_count = incoming.shape[1]
    dense = dense.reshape(5 * slot_count, table_flat.shape[0])
    result = jnp.dot(
        dense, table_flat, precision=lax.Precision.HIGHEST, preferred_element_type=jnp.float32
    )
    return result.reshape(5, slot_count, table_flat.shape[1]).astype(jnp.bfloat16)


def slot_capacity(electrons, slab_count):
    return max(2, (5 * electrons + 4 * slab_count - 1) // (4 * slab_count))


def general_body(fractions, cell_index, slab_owner, spline_table):
    slab_count = lax.axis_size("slab")
    orb_count = lax.axis_size("orb")
    electrons = slab_owner.shape[0]
    capacity = slot_capacity(electrons, slab_count)
    grid_width = spline_table.shape[1]
    orb_local = spline_table.shape[4]
    owners = slab_owner[:, 0]
    columns = jnp.arange(slab_count, dtype=jnp.int32)
    member = (owners[:, None] == columns[None, :]).astype(jnp.int32)
    earlier = jnp.cumsum(member, axis=0) - member
    slot_place = owners * capacity + jnp.sum(earlier * member, axis=1)
    packed = jnp.concatenate([fractions, cell_index.astype(jnp.float32)], axis=0)
    outgoing = jnp.zeros((5, slab_count * capacity), jnp.float32).at[:, slot_place].set(packed)
    outgoing = outgoing.reshape(5, 1, slab_count, capacity)
    spread = lax.all_gather(outgoing, "orb", axis=1, tiled=True)
    arrived = lax.all_to_all(spread, "slab", split_axis=2, concat_axis=2, tiled=True)
    table_flat = spline_table.reshape(grid_width * grid_width * 4, orb_local)
    per_source = jnp.moveaxis(arrived.reshape(5, orb_count, slab_count * capacity), 1, 0)
    blocks = lax.map(lambda incoming: evaluate(incoming, table_flat, grid_width), per_source)
    results = jnp.moveaxis(blocks, 0, 1).reshape(5, orb_count, slab_count, capacity, orb_local)
    returned = lax.all_to_all(results, "slab", split_axis=2, concat_axis=2, tiled=True)
    at_home = lax.all_to_all(returned, "orb", split_axis=1, concat_axis=4, tiled=True)
    flat_home = at_home.reshape(5, slab_count * capacity, at_home.shape[4])
    return jnp.take(flat_home, slot_place, axis=1)


def iota(shape, dim):
    return lax.broadcasted_iota(jnp.int32, shape, dim)


def to_column(row):
    count = row.shape[1]
    spread = jnp.broadcast_to(row, (count, count))
    return jnp.sum(jnp.where(iota((count, count), 0) == iota((count, count), 1), spread, 0.0), axis=1, keepdims=True)


def pack_kernel(fractions_ref, cells_ref, owner_ref, packed_ref):
    electrons = fractions_ref.shape[1]
    owner = owner_ref[...].astype(F32)
    same = to_column(owner) == owner
    before = iota((electrons, electrons), 0) < iota((electrons, electrons), 1)
    slot = jnp.sum(jnp.where(same & before, 1.0, 0.0), axis=0, keepdims=True)
    packed_ref[...] = jnp.full(packed_ref.shape, -1.0, F32)
    packed_ref[0:3, :electrons] = fractions_ref[...]
    packed_ref[3:5, :electrons] = cells_ref[...].astype(F32)
    packed_ref[5:6, :electrons] = owner
    packed_ref[6:7, :electrons] = slot


def split_kernel(planes, table_ref, high_ref, low_ref):
    blocks = high_ref.shape[1] // LANES
    count = table_ref.shape[0] // (blocks * planes)
    for block in range(blocks):
        for plane in range(planes):
            table = table_ref[pl.ds(block * planes + plane, count, stride=blocks * planes), :]
            high = table.astype(BF16)
            rows, lanes = slice(plane * count, (plane + 1) * count), slice(block * LANES, (block + 1) * LANES)
            high_ref[rows, lanes] = high
            low_ref[rows, lanes] = (table - high.astype(F32)).astype(BF16)


def slot_weights(home, slab, slots, grid_width, high_ref, low_ref):
    owner, slot = home[5:6, :], home[6:7, :]
    wanted = jnp.where(owner == slab.astype(F32), slot, -1.0)
    chosen = iota((slots, LANES), 0).astype(F32) == wanted
    lane = iota((slots, LANES), 1)

    def field(index):
        picked = jnp.sum(jnp.where(chosen, home[index : index + 1, :], 0.0), axis=1, keepdims=True)
        return jnp.broadcast_to(picked, (slots, LANES))

    (x_value, x_slope, x_curve), taps_y, taps_z = (spline_taps(field(dim)) for dim in range(3))
    first_y, first_z = field(3).astype(jnp.int32), field(4).astype(jnp.int32)

    def pick(offset, kinds):
        hits = [offset == tap for tap in range(4)]
        picked = []
        for taps in kinds:
            out = jnp.where(hits[3], taps[3], 0.0)
            for tap in (2, 1, 0):
                out = jnp.where(hits[tap], taps[tap], out)
            picked.append(out)
        return picked

    z_value, z_slope, z_curve = pick(((lane & (grid_width - 1)) - first_z) & (grid_width - 1), taps_z)
    per_chunk = LANES // grid_width
    for chunk in range(grid_width // per_chunk):
        offset_y = (chunk * per_chunk + lane // grid_width - first_y) & (grid_width - 1)
        y_value, y_slope, y_curve = pick(offset_y, taps_y)
        plain = y_value * z_value
        with_y = y_slope * z_value
        with_z = y_value * z_slope
        with_both = y_curve * z_value + y_value * z_curve
        for plane in range(4):
            weights = (
                x_value[plane] * plain,
                x_slope[plane] * plain,
                x_value[plane] * with_y,
                x_value[plane] * with_z,
                x_curve[plane] * plain + x_value[plane] * with_both,
            )
            start = plane * grid_width * grid_width + chunk * LANES
            for k, weight in enumerate(weights):
                high = weight.astype(BF16)
                high_ref[k * slots : (k + 1) * slots, start : start + LANES] = high
                low_ref[k * slots : (k + 1) * slots, start : start + LANES] = (weight - high.astype(F32)).astype(BF16)


def contract(weights, table_high, table_low):
    dot = functools.partial(jnp.dot, preferred_element_type=F32)
    high, low = weights[0][...], weights[1][...]
    return dot(high, table_high) + (dot(low, table_high) + dot(high, table_low))


def store_slots(out_ref, first, result, capacity, slots):
    lanes = out_ref.shape[1]
    for band in range(result.shape[1] // lanes):
        for k in range(5):
            start = ((first + band) * 5 + k) * capacity
            count = min(slots, out_ref.shape[0] - start)
            out_ref[start : start + count, :] = result[k * slots : k * slots + count, band * lanes : (band + 1) * lanes].astype(BF16)


def serve_kernel(sizes, places, *refs):
    capacity, slots, grid_width = sizes
    count = len(places)
    tables, homes_refs, outs, weights = refs[:4], refs[4 : -4 - count], refs[-4 - count : -4], refs[-4:]
    slab = lax.axis_index("slab")
    for index in range(count):
        pair = weights[2 * (index % 2) : 2 * (index % 2) + 2]
        which, place = places[index]
        slot_weights(homes_refs[which][place], slab, slots, grid_width, *pair)
        for half in range(2):
            high_ref, low_ref = tables[2 * half : 2 * half + 2]
            width = high_ref.shape[1]
            result = contract(pair, high_ref[...], low_ref[...])
            store_slots(outs[index], half * (width // outs[index].shape[1]), result, capacity, slots)


def place_kernel(capacity, slots, turn, packed_ref, *refs):
    pieces, (out_ref, placed, sems) = refs[:4], refs[-3:]
    slab, orb = lax.axis_index("slab"), lax.axis_index("orb")
    width = out_ref.shape[2] // 4
    electrons = out_ref.shape[1]
    owner = to_column(packed_ref[5:6, :electrons])
    slot = to_column(packed_ref[6:7, :electrons])
    step = jnp.zeros_like(owner)
    for index in range(1, 4):
        step = jnp.where(owner == (slab ^ index).astype(F32), float(index), step)
    wanted = step * float(slots) + slot
    column = iota((electrons, 4 * slots), 1).astype(F32)
    pick = (column == wanted).astype(BF16)
    pick_last = (column == wanted + float(slots - capacity)).astype(BF16)
    total, lanes = pieces[0].shape
    departures = []
    for half in range(2):
        for band in range(width // lanes):
            for k in range(5):
                start = ((half * (width // lanes) + band) * 5 + k) * capacity
                last = start + slots > total
                rows = slice(total - slots, total) if last else slice(start, start + slots)
                stack = jnp.concatenate([piece[rows, :] for piece in pieces], axis=0)
                result = jnp.dot(pick_last if last else pick, stack, preferred_element_type=F32)
                placed[half, k, :, band * lanes : (band + 1) * lanes] = result.astype(BF16)
        start = pl.multiple_of((orb ^ (2 * turn + half)) * width, LANES)
        departure = pltpu.make_async_copy(placed.at[half], out_ref.at[:, :, pl.ds(start, width)], sems.at[half])
        departure.start()
        departures.append(departure)
    for departure in departures:
        departure.wait()


def swap(array, step, count, axes):
    return lax.ppermute(array, axes, [(i, i ^ step) for i in range(count)])


def after(array, *others):
    return lax.optimization_barrier((array, *others))[0]


HBM = pl.BlockSpec(memory_space=pltpu.HBM)
VMEM = pl.BlockSpec(memory_space=pltpu.VMEM)


def small_body(fractions, cell_index, slab_owner, spline_table):
    electrons = slab_owner.shape[0]
    grid_width, planes, orb_local = spline_table.shape[1], spline_table.shape[3], spline_table.shape[4]
    capacity = slot_capacity(electrons, 4)
    slots = -(-capacity // 16) * 16
    bands = 2 * orb_local // BAND
    rows = bands * 5 * capacity
    taps = grid_width * grid_width * planes
    vmem = pltpu.CompilerParams(vmem_limit_bytes=40 * 1024 * 1024)
    blocks = functools.partial(jax.ShapeDtypeStruct, dtype=BF16)
    both_axes = ("slab", "orb")

    partner_table = swap(spline_table, 1, 4, "orb")
    packed = pl.pallas_call(
        pack_kernel, out_shape=jax.ShapeDtypeStruct((8, LANES), F32), name="pack"
    )(fractions, cell_index, slab_owner.reshape(1, electrons))
    def split(table):
        view = table.reshape(grid_width * grid_width, planes, orb_local // LANES, LANES)
        view = view.transpose(0, 2, 1, 3).reshape(taps * orb_local // LANES, LANES)
        return pl.pallas_call(
            functools.partial(split_kernel, planes),
            out_shape=[blocks((taps, orb_local))] * 2,
            compiler_params=vmem,
            name="split",
        )(view)

    def split(table):
        view = table.reshape(grid_width * grid_width, planes, orb_local // LANES, LANES)
        view = view.transpose(0, 2, 1, 3).reshape(taps * orb_local // LANES, LANES)
        return pl.pallas_call(
            functools.partial(split_kernel, planes),
            out_shape=[blocks((taps, orb_local))] * 2,
            compiler_params=vmem,
            name="split",
        )(view)

    along = [packed] + [swap(packed, step, 4, "slab") for step in (1, 2, 3)]
    tables = split(spline_table) + split(partner_table)
    pair = jnp.stack([after(packed, *tables), swap(packed, 2, 4, "slab")])
    side = swap(pair, 1, 4, "slab")

    def serve(name, homes, *places):
        count = len(places)
        return pl.pallas_call(
            functools.partial(serve_kernel, (capacity, slots, grid_width), places),
            out_shape=[blocks((rows, BAND))] * count,
            in_specs=[VMEM] * (4 + len(homes)),
            out_specs=[VMEM] * count,
            scratch_shapes=[pltpu.VMEM((5 * slots, taps), BF16)] * 4,
            compiler_params=vmem,
            name=name,
        )(*tables, *homes)

    def send(step, block):
        return swap(block, step, 16, both_axes)

    across_out = serve("across", [pair], (0, 1))
    straight = jnp.stack([after(pair, *across_out), side])
    crossed = swap(straight, 2, 4, "orb")
    across_out += serve("across", [after(crossed, *across_out)], (0, (0, 1)))
    both = (after(straight, *across_out), crossed)
    corner_out = serve("corner", both, (0, (1, 1)), (1, (1, 1)))
    both = (after(straight, *corner_out), crossed)
    near_out = serve("near", both, (0, (0, 0)), (1, (0, 0)), (0, (1, 0)), (1, (1, 0)))
    far = [send(8 + 2 * index, block) for index, block in enumerate(across_out + corner_out)]
    near = [near_out[0]] + [send(2 * index, near_out[index]) for index in range(1, 4)]
    out = ()
    for turn in range(2):
        pieces = near[turn::2] + far[turn::2]
        out = pl.pallas_call(
            functools.partial(place_kernel, capacity, slots, turn),
            out_shape=[blocks((5, electrons, 4 * orb_local))],
            in_specs=[VMEM] * 5 + [HBM] * len(out),
            out_specs=[HBM],
            input_output_aliases={5: 0} if out else {},
            scratch_shapes=[pltpu.VMEM((2, 5, electrons, orb_local), BF16), pltpu.SemaphoreType.DMA((2,))],
            compiler_params=vmem,
            name="place",
        )(packed, *pieces, *out)
    return out[0]


def solution(mesh):
    in_specs = (
        P(None, ("groups", "slab", "orb")),
        P(None, ("groups", "slab", "orb")),
        P(("groups", "slab", "orb"), None),
        P("slab", None, None, None, "orb"),
    )
    out_specs = P(None, ("groups", "slab", "orb"), None)
    small = (mesh.shape["groups"], mesh.shape["slab"], mesh.shape["orb"]) == (2, 4, 4)
    body = small_body if small else general_body
    return jax.shard_map(body, mesh=mesh, in_specs=in_specs, out_specs=out_specs, check_vma=False)
```

```python
import functools

import jax
import jax.numpy as jnp
from jax import lax
from jax.experimental import pallas as pl
from jax.experimental.pallas import tpu as pltpu
from jax.sharding import PartitionSpec as P

LANES = 128
BAND = 256
F32 = jnp.float32
BF16 = jnp.bfloat16


def spline_taps(position):
    remain = 1.0 - position
    square = position * position
    frac_cube = square * position
    values = (
        remain * remain * remain / 6.0,
        (3.0 * frac_cube - 6.0 * square + 4.0) / 6.0,
        (-3.0 * frac_cube + 3.0 * square + 3.0 * position + 1.0) / 6.0,
        frac_cube / 6.0,
    )
    slopes = (
        -0.5 * remain * remain,
        0.5 * (3.0 * square - 4.0 * position),
        0.5 * (-3.0 * square + 2.0 * position + 1.0),
        0.5 * square,
    )
    curves = (remain, 3.0 * position - 2.0, 1.0 - 3.0 * position, position)
    return values, slopes, curves


def spline_bases(position):
    return tuple(jnp.stack(taps, axis=-1) for taps in spline_taps(position))


def spread_taps(first_cell, taps, grid_width):
    offsets = jnp.arange(4, dtype=jnp.int32)
    cells = jnp.arange(grid_width, dtype=jnp.int32)
    wrapped = (first_cell[:, None] + offsets[None, :]) % grid_width
    hits = (wrapped[:, :, None] == cells[None, None, :]).astype(jnp.float32)
    return jnp.sum(hits * taps[:, :, None], axis=1)


def evaluate(incoming, table_flat, grid_width):
    basis_x, slope_x, curve_x = spline_bases(incoming[0])
    basis_y, slope_y, curve_y = spline_bases(incoming[1])
    basis_z, slope_z, curve_z = spline_bases(incoming[2])
    row_y = incoming[3].astype(jnp.int32)
    row_z = incoming[4].astype(jnp.int32)
    value_y = spread_taps(row_y, basis_y, grid_width)[:, :, None, None]
    deriv_y = spread_taps(row_y, slope_y, grid_width)[:, :, None, None]
    second_y = spread_taps(row_y, curve_y, grid_width)[:, :, None, None]
    value_z = spread_taps(row_z, basis_z, grid_width)[:, None, :, None]
    deriv_z = spread_taps(row_z, slope_z, grid_width)[:, None, :, None]
    second_z = spread_taps(row_z, curve_z, grid_width)[:, None, :, None]
    value_x = basis_x[:, None, None, :]
    deriv_x = slope_x[:, None, None, :]
    second_x = curve_x[:, None, None, :]
    dense = jnp.stack(
        [
            value_x * value_y * value_z,
            deriv_x * value_y * value_z,
            value_x * deriv_y * value_z,
            value_x * value_y * deriv_z,
            second_x * value_y * value_z
            + value_x * second_y * value_z
            + value_x * value_y * second_z,
        ]
    )
    slot_count = incoming.shape[1]
    dense = dense.reshape(5 * slot_count, table_flat.shape[0])
    result = jnp.dot(
        dense, table_flat, precision=lax.Precision.HIGHEST, preferred_element_type=jnp.float32
    )
    return result.reshape(5, slot_count, table_flat.shape[1]).astype(jnp.bfloat16)


def slot_capacity(electrons, slab_count):
    return max(2, (5 * electrons + 4 * slab_count - 1) // (4 * slab_count))


def general_body(fractions, cell_index, slab_owner, spline_table):
    slab_count = lax.axis_size("slab")
    orb_count = lax.axis_size("orb")
    electrons = slab_owner.shape[0]
    capacity = slot_capacity(electrons, slab_count)
    grid_width = spline_table.shape[1]
    orb_local = spline_table.shape[4]
    owners = slab_owner[:, 0]
    columns = jnp.arange(slab_count, dtype=jnp.int32)
    member = (owners[:, None] == columns[None, :]).astype(jnp.int32)
    earlier = jnp.cumsum(member, axis=0) - member
    slot_place = owners * capacity + jnp.sum(earlier * member, axis=1)
    packed = jnp.concatenate([fractions, cell_index.astype(jnp.float32)], axis=0)
    outgoing = jnp.zeros((5, slab_count * capacity), jnp.float32).at[:, slot_place].set(packed)
    outgoing = outgoing.reshape(5, 1, slab_count, capacity)
    spread = lax.all_gather(outgoing, "orb", axis=1, tiled=True)
    arrived = lax.all_to_all(spread, "slab", split_axis=2, concat_axis=2, tiled=True)
    table_flat = spline_table.reshape(grid_width * grid_width * 4, orb_local)
    per_source = jnp.moveaxis(arrived.reshape(5, orb_count, slab_count * capacity), 1, 0)
    blocks = lax.map(lambda incoming: evaluate(incoming, table_flat, grid_width), per_source)
    results = jnp.moveaxis(blocks, 0, 1).reshape(5, orb_count, slab_count, capacity, orb_local)
    returned = lax.all_to_all(results, "slab", split_axis=2, concat_axis=2, tiled=True)
    at_home = lax.all_to_all(returned, "orb", split_axis=1, concat_axis=4, tiled=True)
    flat_home = at_home.reshape(5, slab_count * capacity, at_home.shape[4])
    return jnp.take(flat_home, slot_place, axis=1)


def iota(shape, dim):
    return lax.broadcasted_iota(jnp.int32, shape, dim)


def to_column(row):
    count = row.shape[1]
    spread = jnp.broadcast_to(row, (count, count))
    return jnp.sum(jnp.where(iota((count, count), 0) == iota((count, count), 1), spread, 0.0), axis=1, keepdims=True)


def pack_kernel(fractions_ref, cells_ref, owner_ref, packed_ref):
    electrons = fractions_ref.shape[1]
    owner = owner_ref[...].astype(F32)
    same = to_column(owner) == owner
    before = iota((electrons, electrons), 0) < iota((electrons, electrons), 1)
    slot = jnp.sum(jnp.where(same & before, 1.0, 0.0), axis=0, keepdims=True)
    packed_ref[...] = jnp.full(packed_ref.shape, -1.0, F32)
    packed_ref[0:3, :electrons] = fractions_ref[...]
    packed_ref[3:5, :electrons] = cells_ref[...].astype(F32)
    packed_ref[5:6, :electrons] = owner
    packed_ref[6:7, :electrons] = slot


def split_kernel(planes, table_ref, high_ref, low_ref):
    blocks = high_ref.shape[1] // LANES
    count = table_ref.shape[0] // (blocks * planes)
    for block in range(blocks):
        for plane in range(planes):
            table = table_ref[pl.ds(block * planes + plane, count, stride=blocks * planes), :]
            high = table.astype(BF16)
            rows, lanes = slice(plane * count, (plane + 1) * count), slice(block * LANES, (block + 1) * LANES)
            high_ref[rows, lanes] = high
            low_ref[rows, lanes] = (table - high.astype(F32)).astype(BF16)


def slot_weights(home, slab, slots, grid_width, high_ref, low_ref):
    owner, slot = home[5:6, :], home[6:7, :]
    wanted = jnp.where(owner == slab.astype(F32), slot, -1.0)
    chosen = iota((slots, LANES), 0).astype(F32) == wanted
    lane = iota((slots, LANES), 1)

    def field(index):
        picked = jnp.sum(jnp.where(chosen, home[index : index + 1, :], 0.0), axis=1, keepdims=True)
        return jnp.broadcast_to(picked, (slots, LANES))

    (x_value, x_slope, x_curve), taps_y, taps_z = (spline_taps(field(dim)) for dim in range(3))
    first_y, first_z = field(3).astype(jnp.int32), field(4).astype(jnp.int32)

    def pick(offset, kinds):
        hits = [offset == tap for tap in range(4)]
        picked = []
        for taps in kinds:
            out = jnp.where(hits[3], taps[3], 0.0)
            for tap in (2, 1, 0):
                out = jnp.where(hits[tap], taps[tap], out)
            picked.append(out)
        return picked

    z_value, z_slope, z_curve = pick(((lane & (grid_width - 1)) - first_z) & (grid_width - 1), taps_z)
    per_chunk = LANES // grid_width
    for chunk in range(grid_width // per_chunk):
        offset_y = (chunk * per_chunk + lane // grid_width - first_y) & (grid_width - 1)
        y_value, y_slope, y_curve = pick(offset_y, taps_y)
        plain = y_value * z_value
        with_y = y_slope * z_value
        with_z = y_value * z_slope
        with_both = y_curve * z_value + y_value * z_curve
        for plane in range(4):
            weights = (
                x_value[plane] * plain,
                x_slope[plane] * plain,
                x_value[plane] * with_y,
                x_value[plane] * with_z,
                x_curve[plane] * plain + x_value[plane] * with_both,
            )
            start = plane * grid_width * grid_width + chunk * LANES
            for k, weight in enumerate(weights):
                high = weight.astype(BF16)
                high_ref[k * slots : (k + 1) * slots, start : start + LANES] = high
                low_ref[k * slots : (k + 1) * slots, start : start + LANES] = (weight - high.astype(F32)).astype(BF16)


def contract(weights, table_high, table_low):
    dot = functools.partial(jnp.dot, preferred_element_type=F32)
    high, low = weights[0][...], weights[1][...]
    return dot(high, table_high) + (dot(low, table_high) + dot(high, table_low))


def store_slots(out_ref, first, result, capacity, slots):
    lanes = out_ref.shape[1]
    for band in range(result.shape[1] // lanes):
        for k in range(5):
            start = ((first + band) * 5 + k) * capacity
            count = min(slots, out_ref.shape[0] - start)
            out_ref[start : start + count, :] = result[k * slots : k * slots + count, band * lanes : (band + 1) * lanes].astype(BF16)


def serve_kernel(sizes, places, *refs):
    capacity, slots, grid_width = sizes
    count = len(places)
    tables, homes_refs, outs, weights = refs[:4], refs[4 : -4 - count], refs[-4 - count : -4], refs[-4:]
    slab = lax.axis_index("slab")
    for index in range(count):
        pair = weights[2 * (index % 2) : 2 * (index % 2) + 2]
        which, place = places[index]
        slot_weights(homes_refs[which][place], slab, slots, grid_width, *pair)
        for half in range(2):
            high_ref, low_ref = tables[2 * half : 2 * half + 2]
            width = high_ref.shape[1]
            result = contract(pair, high_ref[...], low_ref[...])
            store_slots(outs[index], half * (width // outs[index].shape[1]), result, capacity, slots)


def place_kernel(capacity, slots, turn, packed_ref, *refs):
    pieces, (out_ref, placed, sems) = refs[:4], refs[-3:]
    slab, orb = lax.axis_index("slab"), lax.axis_index("orb")
    width = out_ref.shape[2] // 4
    electrons = out_ref.shape[1]
    owner = to_column(packed_ref[5:6, :electrons])
    slot = to_column(packed_ref[6:7, :electrons])
    step = jnp.zeros_like(owner)
    for index in range(1, 4):
        step = jnp.where(owner == (slab ^ index).astype(F32), float(index), step)
    wanted = step * float(slots) + slot
    column = iota((electrons, 4 * slots), 1).astype(F32)
    pick = (column == wanted).astype(BF16)
    pick_last = (column == wanted + float(slots - capacity)).astype(BF16)
    total, lanes = pieces[0].shape
    departures = []
    for half in range(2):
        for band in range(width // lanes):
            for k in range(5):
                start = ((half * (width // lanes) + band) * 5 + k) * capacity
                last = start + slots > total
                rows = slice(total - slots, total) if last else slice(start, start + slots)
                stack = jnp.concatenate([piece[rows, :] for piece in pieces], axis=0)
                result = jnp.dot(pick_last if last else pick, stack, preferred_element_type=F32)
                placed[half, k, :, band * lanes : (band + 1) * lanes] = result.astype(BF16)
            start = pl.multiple_of((orb ^ (2 * turn + half)) * width + band * lanes, LANES)
            source = placed.at[half, :, :, band * lanes : (band + 1) * lanes]
            departure = pltpu.make_async_copy(source, out_ref.at[:, :, pl.ds(start, lanes)], sems.at[half * (width // lanes) + band])
            departure.start()
            departures.append(departure)
    for departure in departures:
        departure.wait()


def swap(array, step, count, axes):
    return lax.ppermute(array, axes, [(i, i ^ step) for i in range(count)])


def after(array, *others):
    return lax.optimization_barrier((array, *others))[0]


HBM = pl.BlockSpec(memory_space=pltpu.HBM)
VMEM = pl.BlockSpec(memory_space=pltpu.VMEM)


def small_body(fractions, cell_index, slab_owner, spline_table):
    electrons = slab_owner.shape[0]
    grid_width, planes, orb_local = spline_table.shape[1], spline_table.shape[3], spline_table.shape[4]
    capacity = slot_capacity(electrons, 4)
    slots = -(-capacity // 16) * 16
    bands = 2 * orb_local // BAND
    rows = bands * 5 * capacity
    taps = grid_width * grid_width * planes
    vmem = pltpu.CompilerParams(vmem_limit_bytes=40 * 1024 * 1024)
    blocks = functools.partial(jax.ShapeDtypeStruct, dtype=BF16)
    both_axes = ("slab", "orb")

    partner_table = swap(spline_table, 1, 4, "orb")
    packed = pl.pallas_call(
        pack_kernel, out_shape=jax.ShapeDtypeStruct((8, LANES), F32), name="pack"
    )(fractions, cell_index, slab_owner.reshape(1, electrons))

    def split(table):
        view = table.reshape(grid_width * grid_width, planes, orb_local // LANES, LANES)
        view = view.transpose(0, 2, 1, 3).reshape(taps * orb_local // LANES, LANES)
        return pl.pallas_call(
            functools.partial(split_kernel, planes),
            out_shape=[blocks((taps, orb_local))] * 2,
            compiler_params=vmem,
            name="split",
        )(view)

    tables = split(spline_table) + split(partner_table)
    pair = jnp.stack([after(packed, *tables), swap(packed, 2, 4, "slab")])
    side = swap(pair, 1, 4, "slab")

    def serve(name, homes, *places):
        count = len(places)
        return pl.pallas_call(
            functools.partial(serve_kernel, (capacity, slots, grid_width), places),
            out_shape=[blocks((rows, BAND))] * count,
            in_specs=[VMEM] * (4 + len(homes)),
            out_specs=[VMEM] * count,
            scratch_shapes=[pltpu.VMEM((5 * slots, taps), BF16)] * 4,
            compiler_params=vmem,
            name=name,
        )(*tables, *homes)

    def send(step, block):
        return swap(block, step, 16, both_axes)

    across_out = serve("across", [pair], (0, 1))
    straight = jnp.stack([after(pair, *across_out), side])
    crossed = swap(straight, 2, 4, "orb")
    across_out += serve("across", [after(crossed, *across_out)], (0, (0, 1)))
    both = (after(straight, *across_out), crossed)
    corner_out = serve("corner", both, (0, (1, 1)), (1, (1, 1)))
    both = (after(straight, *corner_out), crossed)
    near_out = serve("near", both, (0, (0, 0)), (1, (0, 0)), (0, (1, 0)), (1, (1, 0)))
    far = [send(8 + 2 * index, block) for index, block in enumerate(across_out + corner_out)]
    near = [near_out[0]] + [send(2 * index, near_out[index]) for index in range(1, 4)]
    out = ()
    for turn in range(2):
        pieces = near[turn::2] + far[turn::2]
        out = pl.pallas_call(
            functools.partial(place_kernel, capacity, slots, turn),
            out_shape=[blocks((5, electrons, 4 * orb_local))],
            in_specs=[VMEM] * 5 + [HBM] * len(out),
            out_specs=[HBM],
            input_output_aliases={5: 0} if out else {},
            scratch_shapes=[pltpu.VMEM((2, 5, electrons, orb_local), BF16), pltpu.SemaphoreType.DMA((bands,))],
            compiler_params=vmem,
            name="place",
        )(packed, *pieces, *out)
    return out[0]


def solution(mesh):
    in_specs = (
        P(None, ("groups", "slab", "orb")),
        P(None, ("groups", "slab", "orb")),
        P(("groups", "slab", "orb"), None),
        P("slab", None, None, None, "orb"),
    )
    out_specs = P(None, ("groups", "slab", "orb"), None)
    small = (mesh.shape["groups"], mesh.shape["slab"], mesh.shape["orb"]) == (2, 4, 4)
    body = small_body if small else general_body
    return jax.shard_map(body, mesh=mesh, in_specs=in_specs, out_specs=out_specs, check_vma=False)
```

```python
import functools

import jax
import jax.numpy as jnp
from jax import lax
from jax.experimental import pallas as pl
from jax.experimental.pallas import tpu as pltpu
from jax.sharding import PartitionSpec as P

LANES = 128
BAND = 256
F32 = jnp.float32
BF16 = jnp.bfloat16


def spline_taps(position):
    remain = 1.0 - position
    square = position * position
    frac_cube = square * position
    values = (
        remain * remain * remain / 6.0,
        (3.0 * frac_cube - 6.0 * square + 4.0) / 6.0,
        (-3.0 * frac_cube + 3.0 * square + 3.0 * position + 1.0) / 6.0,
        frac_cube / 6.0,
    )
    slopes = (
        -0.5 * remain * remain,
        0.5 * (3.0 * square - 4.0 * position),
        0.5 * (-3.0 * square + 2.0 * position + 1.0),
        0.5 * square,
    )
    curves = (remain, 3.0 * position - 2.0, 1.0 - 3.0 * position, position)
    return values, slopes, curves


def spline_bases(position):
    return tuple(jnp.stack(taps, axis=-1) for taps in spline_taps(position))


def spread_taps(first_cell, taps, grid_width):
    offsets = jnp.arange(4, dtype=jnp.int32)
    cells = jnp.arange(grid_width, dtype=jnp.int32)
    wrapped = (first_cell[:, None] + offsets[None, :]) % grid_width
    hits = (wrapped[:, :, None] == cells[None, None, :]).astype(jnp.float32)
    return jnp.sum(hits * taps[:, :, None], axis=1)


def evaluate(incoming, table_flat, grid_width):
    basis_x, slope_x, curve_x = spline_bases(incoming[0])
    basis_y, slope_y, curve_y = spline_bases(incoming[1])
    basis_z, slope_z, curve_z = spline_bases(incoming[2])
    row_y = incoming[3].astype(jnp.int32)
    row_z = incoming[4].astype(jnp.int32)
    value_y = spread_taps(row_y, basis_y, grid_width)[:, :, None, None]
    deriv_y = spread_taps(row_y, slope_y, grid_width)[:, :, None, None]
    second_y = spread_taps(row_y, curve_y, grid_width)[:, :, None, None]
    value_z = spread_taps(row_z, basis_z, grid_width)[:, None, :, None]
    deriv_z = spread_taps(row_z, slope_z, grid_width)[:, None, :, None]
    second_z = spread_taps(row_z, curve_z, grid_width)[:, None, :, None]
    value_x = basis_x[:, None, None, :]
    deriv_x = slope_x[:, None, None, :]
    second_x = curve_x[:, None, None, :]
    dense = jnp.stack(
        [
            value_x * value_y * value_z,
            deriv_x * value_y * value_z,
            value_x * deriv_y * value_z,
            value_x * value_y * deriv_z,
            second_x * value_y * value_z
            + value_x * second_y * value_z
            + value_x * value_y * second_z,
        ]
    )
    slot_count = incoming.shape[1]
    dense = dense.reshape(5 * slot_count, table_flat.shape[0])
    result = jnp.dot(
        dense, table_flat, precision=lax.Precision.HIGHEST, preferred_element_type=jnp.float32
    )
    return result.reshape(5, slot_count, table_flat.shape[1]).astype(jnp.bfloat16)


def slot_capacity(electrons, slab_count):
    return max(2, (5 * electrons + 4 * slab_count - 1) // (4 * slab_count))


def general_body(fractions, cell_index, slab_owner, spline_table):
    slab_count = lax.axis_size("slab")
    orb_count = lax.axis_size("orb")
    electrons = slab_owner.shape[0]
    capacity = slot_capacity(electrons, slab_count)
    grid_width = spline_table.shape[1]
    orb_local = spline_table.shape[4]
    owners = slab_owner[:, 0]
    columns = jnp.arange(slab_count, dtype=jnp.int32)
    member = (owners[:, None] == columns[None, :]).astype(jnp.int32)
    earlier = jnp.cumsum(member, axis=0) - member
    slot_place = owners * capacity + jnp.sum(earlier * member, axis=1)
    packed = jnp.concatenate([fractions, cell_index.astype(jnp.float32)], axis=0)
    outgoing = jnp.zeros((5, slab_count * capacity), jnp.float32).at[:, slot_place].set(packed)
    outgoing = outgoing.reshape(5, 1, slab_count, capacity)
    spread = lax.all_gather(outgoing, "orb", axis=1, tiled=True)
    arrived = lax.all_to_all(spread, "slab", split_axis=2, concat_axis=2, tiled=True)
    table_flat = spline_table.reshape(grid_width * grid_width * 4, orb_local)
    per_source = jnp.moveaxis(arrived.reshape(5, orb_count, slab_count * capacity), 1, 0)
    blocks = lax.map(lambda incoming: evaluate(incoming, table_flat, grid_width), per_source)
    results = jnp.moveaxis(blocks, 0, 1).reshape(5, orb_count, slab_count, capacity, orb_local)
    returned = lax.all_to_all(results, "slab", split_axis=2, concat_axis=2, tiled=True)
    at_home = lax.all_to_all(returned, "orb", split_axis=1, concat_axis=4, tiled=True)
    flat_home = at_home.reshape(5, slab_count * capacity, at_home.shape[4])
    return jnp.take(flat_home, slot_place, axis=1)


def iota(shape, dim):
    return lax.broadcasted_iota(jnp.int32, shape, dim)


def to_column(row):
    count = row.shape[1]
    spread = jnp.broadcast_to(row, (count, count))
    return jnp.sum(jnp.where(iota((count, count), 0) == iota((count, count), 1), spread, 0.0), axis=1, keepdims=True)


def pack_kernel(fractions_ref, cells_ref, owner_ref, packed_ref):
    electrons = fractions_ref.shape[1]
    owner = owner_ref[...].astype(F32)
    same = to_column(owner) == owner
    before = iota((electrons, electrons), 0) < iota((electrons, electrons), 1)
    slot = jnp.sum(jnp.where(same & before, 1.0, 0.0), axis=0, keepdims=True)
    packed_ref[...] = jnp.full(packed_ref.shape, -1.0, F32)
    packed_ref[0:3, :electrons] = fractions_ref[...]
    packed_ref[3:5, :electrons] = cells_ref[...].astype(F32)
    packed_ref[5:6, :electrons] = owner
    packed_ref[6:7, :electrons] = slot


def split_kernel(planes, table_ref, high_ref, low_ref):
    blocks = high_ref.shape[1] // LANES
    count = table_ref.shape[0] // (blocks * planes)
    for block in range(blocks):
        for plane in range(planes):
            table = table_ref[pl.ds(block * planes + plane, count, stride=blocks * planes), :]
            high = table.astype(BF16)
            rows, lanes = slice(plane * count, (plane + 1) * count), slice(block * LANES, (block + 1) * LANES)
            high_ref[rows, lanes] = high
            low_ref[rows, lanes] = (table - high.astype(F32)).astype(BF16)


def slot_weights(home, slab, slots, grid_width, high_ref, low_ref):
    owner, slot = home[5:6, :], home[6:7, :]
    wanted = jnp.where(owner == slab.astype(F32), slot, -1.0)
    chosen = iota((slots, LANES), 0).astype(F32) == wanted
    lane = iota((slots, LANES), 1)

    def field(index):
        picked = jnp.sum(jnp.where(chosen, home[index : index + 1, :], 0.0), axis=1, keepdims=True)
        return jnp.broadcast_to(picked, (slots, LANES))

    (x_value, x_slope, x_curve), taps_y, taps_z = (spline_taps(field(dim)) for dim in range(3))
    first_y, first_z = field(3).astype(jnp.int32), field(4).astype(jnp.int32)

    def pick(offset, kinds):
        hits = [offset == tap for tap in range(4)]
        picked = []
        for taps in kinds:
            out = jnp.where(hits[3], taps[3], 0.0)
            for tap in (2, 1, 0):
                out = jnp.where(hits[tap], taps[tap], out)
            picked.append(out)
        return picked

    z_value, z_slope, z_curve = pick(((lane & (grid_width - 1)) - first_z) & (grid_width - 1), taps_z)
    per_chunk = LANES // grid_width
    for chunk in range(grid_width // per_chunk):
        offset_y = (chunk * per_chunk + lane // grid_width - first_y) & (grid_width - 1)
        y_value, y_slope, y_curve = pick(offset_y, taps_y)
        plain = y_value * z_value
        with_y = y_slope * z_value
        with_z = y_value * z_slope
        with_both = y_curve * z_value + y_value * z_curve
        for plane in range(4):
            weights = (
                x_value[plane] * plain,
                x_slope[plane] * plain,
                x_value[plane] * with_y,
                x_value[plane] * with_z,
                x_curve[plane] * plain + x_value[plane] * with_both,
            )
            start = plane * grid_width * grid_width + chunk * LANES
            for k, weight in enumerate(weights):
                high = weight.astype(BF16)
                high_ref[k * slots : (k + 1) * slots, start : start + LANES] = high
                low_ref[k * slots : (k + 1) * slots, start : start + LANES] = (weight - high.astype(F32)).astype(BF16)


def contract(weights, table_high, table_low):
    dot = functools.partial(jnp.dot, preferred_element_type=F32)
    high, low = weights[0][...], weights[1][...]
    both = dot(high, jnp.concatenate([table_high, table_low], axis=1))
    width = table_high.shape[1]
    return both[:, :width] + (dot(low, table_high) + both[:, width:])


def store_slots(out_ref, first, result, capacity, slots):
    lanes = out_ref.shape[1]
    for band in range(result.shape[1] // lanes):
        for k in range(5):
            start = ((first + band) * 5 + k) * capacity
            count = min(slots, out_ref.shape[0] - start)
            out_ref[start : start + count, :] = result[k * slots : k * slots + count, band * lanes : (band + 1) * lanes].astype(BF16)


def serve_kernel(sizes, places, *refs):
    capacity, slots, grid_width = sizes
    count = len(places)
    tables, homes_refs, outs, weights = refs[:4], refs[4 : -4 - count], refs[-4 - count : -4], refs[-4:]
    slab = lax.axis_index("slab")
    for index in range(count):
        pair = weights[2 * (index % 2) : 2 * (index % 2) + 2]
        which, place = places[index]
        slot_weights(homes_refs[which][place], slab, slots, grid_width, *pair)
        for half in range(2):
            high_ref, low_ref = tables[2 * half : 2 * half + 2]
            width = high_ref.shape[1]
            result = contract(pair, high_ref[...], low_ref[...])
            store_slots(outs[index], half * (width // outs[index].shape[1]), result, capacity, slots)


def place_kernel(capacity, slots, turn, packed_ref, *refs):
    pieces, (out_ref, placed, sems) = refs[:4], refs[-3:]
    slab, orb = lax.axis_index("slab"), lax.axis_index("orb")
    width = out_ref.shape[2] // 4
    electrons = out_ref.shape[1]
    owner = to_column(packed_ref[5:6, :electrons])
    slot = to_column(packed_ref[6:7, :electrons])
    step = jnp.zeros_like(owner)
    for index in range(1, 4):
        step = jnp.where(owner == (slab ^ index).astype(F32), float(index), step)
    wanted = step * float(slots) + slot
    column = iota((electrons, 4 * slots), 1).astype(F32)
    pick = (column == wanted).astype(BF16)
    pick_last = (column == wanted + float(slots - capacity)).astype(BF16)
    total, lanes = pieces[0].shape
    departures = []
    for half in range(2):
        for band in range(width // lanes):
            for k in range(5):
                start = ((half * (width // lanes) + band) * 5 + k) * capacity
                last = start + slots > total
                rows = slice(total - slots, total) if last else slice(start, start + slots)
                stack = jnp.concatenate([piece[rows, :] for piece in pieces], axis=0)
                result = jnp.dot(pick_last if last else pick, stack, preferred_element_type=F32)
                placed[half, k, :, band * lanes : (band + 1) * lanes] = result.astype(BF16)
            start = pl.multiple_of((orb ^ (2 * turn + half)) * width + band * lanes, LANES)
            source = placed.at[half, :, :, band * lanes : (band + 1) * lanes]
            departure = pltpu.make_async_copy(source, out_ref.at[:, :, pl.ds(start, lanes)], sems.at[half * (width // lanes) + band])
            departure.start()
            departures.append(departure)
    for departure in departures:
        departure.wait()


def swap(array, step, count, axes):
    return lax.ppermute(array, axes, [(i, i ^ step) for i in range(count)])


def after(array, *others):
    return lax.optimization_barrier((array, *others))[0]


HBM = pl.BlockSpec(memory_space=pltpu.HBM)
VMEM = pl.BlockSpec(memory_space=pltpu.VMEM)


def small_body(fractions, cell_index, slab_owner, spline_table):
    electrons = slab_owner.shape[0]
    grid_width, planes, orb_local = spline_table.shape[1], spline_table.shape[3], spline_table.shape[4]
    capacity = slot_capacity(electrons, 4)
    slots = -(-capacity // 16) * 16
    bands = 2 * orb_local // BAND
    rows = bands * 5 * capacity
    taps = grid_width * grid_width * planes
    vmem = pltpu.CompilerParams(vmem_limit_bytes=40 * 1024 * 1024)
    blocks = functools.partial(jax.ShapeDtypeStruct, dtype=BF16)
    both_axes = ("slab", "orb")

    partner_table = swap(spline_table, 1, 4, "orb")
    packed = pl.pallas_call(
        pack_kernel, out_shape=jax.ShapeDtypeStruct((8, LANES), F32), name="pack"
    )(fractions, cell_index, slab_owner.reshape(1, electrons))

    def split(table):
        view = table.reshape(grid_width * grid_width, planes, orb_local // LANES, LANES)
        view = view.transpose(0, 2, 1, 3).reshape(taps * orb_local // LANES, LANES)
        return pl.pallas_call(
            functools.partial(split_kernel, planes),
            out_shape=[blocks((taps, orb_local))] * 2,
            compiler_params=vmem,
            name="split",
        )(view)

    tables = split(spline_table) + split(partner_table)
    pair = jnp.stack([after(packed, *tables), swap(packed, 2, 4, "slab")])
    side = swap(pair, 1, 4, "slab")

    def serve(name, homes, *places):
        count = len(places)
        return pl.pallas_call(
            functools.partial(serve_kernel, (capacity, slots, grid_width), places),
            out_shape=[blocks((rows, BAND))] * count,
            in_specs=[VMEM] * (4 + len(homes)),
            out_specs=[VMEM] * count,
            scratch_shapes=[pltpu.VMEM((5 * slots, taps), BF16)] * 4,
            compiler_params=vmem,
            name=name,
        )(*tables, *homes)

    def send(step, block):
        return swap(block, step, 16, both_axes)

    across_out = serve("across", [pair], (0, 1))
    straight = jnp.stack([after(pair, *across_out), side])
    crossed = swap(straight, 2, 4, "orb")
    across_out += serve("across", [after(crossed, *across_out)], (0, (0, 1)))
    both = (after(straight, *across_out), crossed)
    corner_out = serve("corner", both, (0, (1, 1)), (1, (1, 1)))
    both = (after(straight, *corner_out), crossed)
    near_out = serve("near", both, (0, (0, 0)), (1, (0, 0)), (0, (1, 0)), (1, (1, 0)))
    far = [send(8 + 2 * index, block) for index, block in enumerate(across_out + corner_out)]
    near = [near_out[0]] + [send(2 * index, near_out[index]) for index in range(1, 4)]
    out = ()
    for turn in range(2):
        pieces = near[turn::2] + far[turn::2]
        out = pl.pallas_call(
            functools.partial(place_kernel, capacity, slots, turn),
            out_shape=[blocks((5, electrons, 4 * orb_local))],
            in_specs=[VMEM] * 5 + [HBM] * len(out),
            out_specs=[HBM],
            input_output_aliases={5: 0} if out else {},
            scratch_shapes=[pltpu.VMEM((2, 5, electrons, orb_local), BF16), pltpu.SemaphoreType.DMA((bands,))],
            compiler_params=vmem,
            name="place",
        )(packed, *pieces, *out)
    return out[0]


def solution(mesh):
    in_specs = (
        P(None, ("groups", "slab", "orb")),
        P(None, ("groups", "slab", "orb")),
        P(("groups", "slab", "orb"), None),
        P("slab", None, None, None, "orb"),
    )
    out_specs = P(None, ("groups", "slab", "orb"), None)
    small = (mesh.shape["groups"], mesh.shape["slab"], mesh.shape["orb"]) == (2, 4, 4)
    body = small_body if small else general_body
    return jax.shard_map(body, mesh=mesh, in_specs=in_specs, out_specs=out_specs, check_vma=False)
```
